128 devices in a mesh: gx: 16 (over z, y_hi, core), gy: 8 (over x, y_lo).
Axes of the slice: x: 4, y: 4 (y_hi: 2, y_lo: 2; y = y_hi * 2 + y_lo), z: 4, core: 2. Of those that a mesh axis runs over, the one named last changes fastest.
Arguments:
- blocks: bfloat16 [2, 16384, 2048], P(None, ('gx', 'gy')), may hold values from 0.19921875 to 4
- owner_route: int32 [2, 16384, 1], P(None, ('gx', 'gy')), may hold values from 0 to 127; in each aligned block of 128 rows (0 to 127, 128 to 255, ..., all dimensions but the last counted through in order) at most 2 rows name the same one
- block_slot: int32 [2, 16384], P(None, ('gx', 'gy')), may hold values from 0 to 63
- estimate: float32 [2, 4096, 2048], P(None, 'gx', 'gy'), may hold values from 0.5 to 2
- background: float32 [2, 2], replicated, may hold values from 0.2 to 2
- psf_taps: float32 [2, 4, 2, 17], replicated, may hold values from 0.05 to 1
- psf_index: int32 [2, 2], replicated, may hold values from 0 to 3
Outputs:
- deconvolved: float32 [2, 4096, 2048], P(None, 'gx', 'gy')
The draws below stay inside these ranges and needn't reach their ends.
Inputs may be any that keep to these rules, and one draw needn't show every extreme that they name: `owner_route`: among the 128 blocks of one view held by one device (aligned runs of rows along dimension 1), no tile is named more than 2 times.
All inputs are finite; a program needn't handle non-finite values.
Results may differ from the reference program's by a relative error of at most 0.0008.
Values may be sent and summed in bfloat16 or wider, within the bound.
A program may use at most 64 MiB of HBM per device.

```python
import math
import jax
import jax.numpy as jnp
import numpy as np

Z = 2
TX = 256
TY = 256
BS = 32
R = 8
KERNELS = 4
ITERS = 2
BLOCKS_DEV = 128
TAPS = 17
CAP = 2
SPT = 64
CELLS = 2048
BLOCKS = 16384
NX = 4096
NY = 2048
N_GX = 16
N_GY = 8
DEVICES = 128


def plant(values, stream_key, smallest, top_value):
    shape = values.shape
    place = [jax.random.randint(jax.random.fold_in(stream_key, axis), (), 0, shape[axis]) for axis in range(len(shape))]
    values = values.at[tuple(place)].set(smallest)
    longest = shape.index(max(shape))
    place[longest] = (place[longest] + 1) % shape[longest]
    return values.at[tuple(place)].set(top_value)


def block_levels(key, dims, shards, smallest, top_value):
    factor_of, own = 1.0, jax.random.fold_in(key, 6)
    for axis_at, parts in shards:
        steps = jnp.exp(jax.random.uniform(jax.random.fold_in(own, axis_at), (parts,), jnp.float32, smallest / len(shards), top_value / len(shards)))
        factor_of = factor_of * jnp.repeat(steps, dims[axis_at] // parts).reshape([-1 if axis == axis_at else 1 for axis in range(len(dims))])
    return factor_of


def assign_block(key, own, number, rows, count, top, limit, lean):
    ranking = jax.random.permutation(key, count)
    crowded, ordinary = shares(count, rows * top, limit, lean, True), shares(count, rows * top, limit, lean, False)
    places = jnp.arange(count)

    def named(sizes, rotation):
        used = int((sizes > 0).sum())
        fixed = max(1, used // 4)
        shifted = fixed + (places - fixed + rotation * (used - fixed)) % max(1, count - fixed)
        return jnp.zeros((count,), jnp.int32).at[ranking[jnp.where(places < fixed, places, shifted)]].set(jnp.asarray(sizes, jnp.int32))

    sizes = jnp.where(number % 4 == 0, named(crowded, number // 4), named(ordinary, number - number // 4 - 1))
    mixed = jax.random.permutation(jax.random.fold_in(own, 3), count)
    donor, sink = mixed[0:count // 2 * 2:2], mixed[1:count // 2 * 2:2]
    margin = jnp.minimum(sizes[donor] - 1, limit - sizes[sink]) // 2
    margin = jnp.where((donor == ranking[0]) | (sink == ranking[0]) | (sizes[sink] == 0), 0, jnp.maximum(margin, 0))
    shifted = jax.random.randint(jax.random.fold_in(own, 4), (count // 2,), 0, 1 << 20) % (margin + 1)
    sizes = sizes.at[donor].add(-shifted).at[sink].add(shifted)
    members = jnp.searchsorted(jnp.cumsum(sizes), jnp.arange(rows * top), side="right").astype(jnp.int32)
    listing = members.reshape(top, rows).T
    listing = listing[jax.random.permutation(jax.random.fold_in(own, 1), rows)]
    rotation = jax.random.randint(jax.random.fold_in(own, 2), (rows, 1), 0, top)
    return jnp.take_along_axis(listing, (jnp.arange(top)[None, :] + rotation) % top, axis=1)


def shares(number_of, total, bound, slope, full):
    loads = [(1 << 20) // math.isqrt(rank ** slope) + 1 for rank in range(1, number_of + 1)]
    largest = bound if full else min(bound, max(-(-total // number_of), total * loads[0] // sum(loads)))
    least = 1 if total - largest >= number_of - 1 else 0
    given, spare = [largest] + [least] * (number_of - 1), total - largest - least * (number_of - 1)
    while spare > 0:
        free = [i for i in range(1, number_of) if given[i] < largest] or [i for i in range(1, number_of) if given[i] < bound]
        pool, remaining = sum([loads[i] for i in free]), spare
        for i in free:
            addition = min(bound - given[i], max(1, remaining * loads[i] // pool), spare)
            given[i] = given[i] + addition
            spare = spare - addition
    return np.array(given)


def setup_inputs(seed: int = 0) -> dict:
    keys = jax.random.split(jax.random.key(seed), 8)
    blocks = jnp.clip(jnp.exp(math.log(4.0) - 2.9996462 * jax.random.uniform(keys[0], (2, BLOCKS, CELLS), jnp.float32) ** block_levels(keys[0], (2, BLOCKS, CELLS), ((1, 128),), -0.2, 0.2)), 0.19921875, 4.0).astype(jnp.bfloat16)
    owner_route_keys = jax.random.split(jax.random.fold_in(keys[1], 1), 2 * BLOCKS // BLOCKS_DEV)
    owner_route_turns = jax.random.permutation(jax.random.fold_in(keys[1], 3), 2 * BLOCKS // BLOCKS_DEV)
    owner_route = jax.vmap(lambda own, number: assign_block(jax.random.fold_in(keys[1], 2), own, number, BLOCKS_DEV, DEVICES, 1, CAP, 2))(owner_route_keys, owner_route_turns).reshape((2, BLOCKS, 1))
    block_slot = plant(jax.random.randint(keys[2], (2, BLOCKS), 0, SPT), jax.random.fold_in(keys[2], 1), 0, SPT - 1).astype(jnp.int32)
    estimate = jnp.clip(jnp.exp(math.log(2.0) - 1.3862944 * jax.random.uniform(keys[3], (Z, NX, NY), jnp.float32) ** block_levels(keys[3], (Z, NX, NY), ((1, 16), (2, 8)), -0.2, 0.2)), 0.5, 2.0)
    background = jnp.clip(jnp.exp(jax.random.uniform(keys[4], (2, Z), jnp.float32, math.log(0.2), math.log(2.0))), 0.2, 2.0)
    psf_taps = jnp.clip(jnp.exp(jax.random.uniform(keys[5], (2, KERNELS, 2, TAPS), jnp.float32, math.log(0.05), math.log(1.0))), 0.05, 1.0)
    psf_index = plant(jax.random.randint(keys[6], (2, Z), 0, KERNELS), jax.random.fold_in(keys[6], 1), 0, KERNELS - 1).astype(jnp.int32)
    return {"blocks": blocks, "owner_route": owner_route, "block_slot": block_slot, "estimate": estimate, "background": background, "psf_taps": psf_taps, "psf_index": psf_index}


def plane_kernels(psf_taps, psf_index):
    normed = psf_taps / jnp.sum(psf_taps, axis=-1, keepdims=True)
    return jnp.stack([normed[0][psf_index[0]], normed[1][psf_index[1]]])


def apply_blur(field, kernels):
    extent_x = field.shape[1]
    extent_y = field.shape[2]
    padded = jnp.pad(field, ((0, 0), (R, R), (0, 0)))
    along_x = jnp.zeros(field.shape, jnp.float32)
    for tap_index in range(2 * R + 1):
        along_x = along_x + kernels[:, 0, tap_index][:, None, None] * padded[:, tap_index:tap_index + extent_x, :]
    padded = jnp.pad(along_x, ((0, 0), (0, 0), (R, R)))
    result = jnp.zeros(field.shape, jnp.float32)
    for tap_index in range(2 * R + 1):
        result = result + kernels[:, 1, tap_index][:, None, None] * padded[:, :, tap_index:tap_index + extent_y]
    return result


def measured_views(blocks, owner_route, block_slot):
    spot_count = (TX // BS) * (TY // BS)
    grids = []
    for view_index in range(2):
        target = owner_route[view_index, :, 0] * spot_count + block_slot[view_index]
        summed = jax.ops.segment_sum(blocks[view_index].astype(jnp.float32), target, num_segments=N_GX * N_GY * spot_count)
        grid = summed.reshape(N_GX, N_GY, TX // BS, TY // BS, Z, BS, BS)
        grids.append(grid.transpose(4, 0, 2, 5, 1, 3, 6).reshape(Z, NX, NY))
    return grids


def reference(blocks, owner_route, block_slot, estimate, background, psf_taps, psf_index):
    measured = measured_views(blocks, owner_route, block_slot)
    kernels = plane_kernels(psf_taps, psf_index)
    flipped = kernels[..., ::-1]
    current = estimate
    for iteration in range(ITERS):
        correction = jnp.zeros(current.shape, jnp.float32)
        for view_index in range(2):
            forward = apply_blur(current, kernels[view_index])
            ratios_here = measured[view_index] / (forward + background[view_index][:, None, None])
            correction = correction + apply_blur(ratios_here, flipped[view_index])
        current = current * (0.5 * correction)
    return current
```

```python
import jax
import jax.numpy as jnp
from jax import lax
from jax.experimental import pallas as pl
from jax.experimental.pallas import tpu as pltpu
from jax.sharding import PartitionSpec as P

MESH = pl.DeviceIdType.MESH
F32 = jnp.float32
BF16 = jnp.bfloat16

N_GX, N_GY = 16, 8
DEVICES = N_GX * N_GY
TILE = 256
TAPS = 17
STEP, STEP_INVERSE = 27, 19
GROUP = 16
GROUPS = DEVICES // GROUP
CHUNK = 8
HALO_PARTS = (
    (0, 32, 1, 0),
    (32, 32, -1, 0),
    (64, 64, 0, 1),
    (128, 64, 0, -1),
    (192, 16, 1, 1),
    (208, 16, 1, -1),
    (224, 16, -1, 1),
    (240, 16, -1, -1),
)
HALO_ROWS = 256


def iota(shape, dim):
    return lax.broadcasted_iota(jnp.int32, shape, dim)


def dot(a, b):
    return jnp.dot(a, b, preferred_element_type=F32)


def split(a):
    high = a.astype(BF16)
    return high, (a - high.astype(F32)).astype(BF16)


def torus_position():
    gx, gy = lax.axis_index("gx"), lax.axis_index("gy")
    return gy // 2, ((gx // 2) % 2) * 2 + gy % 2, gx // 4, gx % 2


def partner(slot, here):
    x, y, z, core = here
    shift = (slot * STEP) % DEVICES
    core = (core + shift % 2) % 2
    x = (x + (shift // 2) % 4) % 4
    y = (y + (shift // 8) % 4) % 4
    z = (z + shift // 32) % 4
    return z * 4 + (y // 2) * 2 + core, x * 2 + y % 2


def slot_of(tile, here):
    x, y, z, core = here
    gx, gy = tile >> 3, tile & 7
    d_core = ((gx & 1) - core) & 1
    dx = ((gy >> 1) - x) & 3
    dy = ((((gx >> 1) & 1) * 2 + (gy & 1)) - y) & 3
    dz = ((gx >> 2) - z) & 3
    return ((d_core + 2 * dx + 8 * dy + 32 * dz) * STEP_INVERSE) & (DEVICES - 1)


def kernel(
    blocks,
    owners,
    places,
    estimate,
    background,
    psf_taps,
    psf_index,
    result,
    staged,
    outgoing,
    incoming,
    ids_out,
    ids_in,
    landing,
    summed,
    measured,
    inverse,
    ratio,
    shuffle,
    halo_out,
    halo_in,
    fwd_y,
    fwd_y_halo,
    fwd_x,
    fwd_x_halo,
    back_y,
    back_y_halo,
    back_x,
    back_x_halo,
    ready,
    data_sent,
    data_here,
    ids_sent,
    ids_here,
    halo_sent,
    halo_here,
):
    gx, gy = lax.axis_index("gx"), lax.axis_index("gy")
    here = torus_position()
    barrier = pltpu.get_barrier_semaphore()

    for step in range(1, N_GX):
        pl.semaphore_signal(
            barrier, inc=1, device_id=((gx + step) % N_GX, gy), device_id_type=MESH
        )
    for step in range(1, N_GY):
        pl.semaphore_signal(
            barrier, inc=1, device_id=(gx, (gy + step) % N_GY), device_id_type=MESH
        )

    def halo_copy(part, exchange, plane):
        start, rows, to_x, to_y = part
        return pltpu.make_async_remote_copy(
            src_ref=halo_out.at[exchange, plane, pl.ds(start, rows)],
            dst_ref=halo_in.at[exchange, plane, pl.ds(start, rows)],
            send_sem=halo_sent.at[exchange, plane],
            recv_sem=halo_here.at[exchange, plane],
            device_id=((gx + to_x + N_GX) % N_GX, (gy + to_y + N_GY) % N_GY),
            device_id_type=MESH,
        )

    def send_halo(exchange, plane):
        for part in HALO_PARTS:
            halo_copy(part, exchange, plane).start()

    def pack_halo(fields, by_rows, exchange, plane):
        count = len(fields)
        out = halo_out.at[exchange, plane]

        def edge(ref, high, tile):
            if by_rows:
                return ref[pl.ds(248 if high else 0, 8), pl.ds(tile * 128, 128)]
            return ref[tile, pl.ds(31 if high else 0, 8, stride=32), :]

        def stack(parts):
            if count == 1:
                parts = parts + [jnp.zeros_like(parts[0])]
            return jnp.concatenate(parts, axis=0).astype(BF16)

        edges = {}
        for high in (True, False):
            for tile in range(2):
                edges[high, tile] = [edge(ref, high, tile) for ref in fields]
        for at, high in ((0, True), (32, False)):
            for tile in range(2):
                out[pl.ds(at + 16 * tile, 16)] = stack(edges[high, tile])
        for at, high_x, high_y in (
            (192, True, True),
            (208, True, False),
            (224, False, True),
            (240, False, False),
        ):
            tile, shift = (1, 8) if high_y else (0, 16)
            out[pl.ds(at, 16)] = stack(
                [
                    pltpu.roll(e, shift + 8 * v, 1)
                    for v, e in enumerate(edges[high_x, tile])
                ]
            )
        lane = iota((64, 128), 1)
        for at, high_y in ((64, True), (128, False)):
            total = jnp.zeros((64, 128), F32)
            for v, ref in enumerate(fields):
                for slab in range(4):
                    rows = pl.ds(64 * slab, 64)
                    if by_rows:
                        piece = ref[rows, pl.ds(128 if high_y else 0, 128)]
                    else:
                        piece = ref[1 if high_y else 0, rows, :]
                    first = 32 * slab + 8 * v + (0 if high_y else 16)
                    moved = pltpu.roll(piece, (first + (8 if high_y else 0)) % 128, 1)
                    total = jnp.where((lane >= first) & (lane < first + 8), moved, total)
            out[pl.ds(at, 64)] = total.astype(BF16)

    def wait_halo(exchange, plane):
        whole = halo_in.at[exchange, plane]
        pltpu.make_async_copy(whole, whole, halo_here.at[exchange, plane]).wait()

    def read_halo(exchange, plane):
        got = halo_in.at[exchange, plane]
        rows = jnp.concatenate(
            [
                jnp.concatenate([got[pl.ds(0, 16)], got[pl.ds(16, 16)]], axis=1),
                jnp.concatenate([got[pl.ds(32, 16)], got[pl.ds(48, 16)]], axis=1),
            ],
            axis=0,
        )
        lane = iota((16, 128), 1)
        corners = [
            jnp.where(
                lane < 16,
                got[pl.ds(at, 16)].astype(F32),
                got[pl.ds(at + 16, 16)].astype(F32),
            )
            for at in (192, 224)
        ]
        lane = iota((64, 128), 1)
        sides = jnp.where(
            lane % 32 < 16, got[pl.ds(64, 64)].astype(F32), got[pl.ds(128, 64)].astype(F32)
        )
        columns = jnp.concatenate(
            [sides] + [pltpu.roll(sides, 128 - 32 * slab, 1) for slab in range(1, 4)] + corners,
            axis=0,
        ).astype(BF16)
        return rows, columns[:, :32]

    slot_rows, rank_rows, rank_columns, place_columns = [], [], [], []
    sub, lane = iota((128, 128), 0), iota((128, 128), 1)
    for v in range(2):
        row = slot_of(owners[pl.ds(v, 1), :], here)
        across = jnp.broadcast_to(row, (128, 128))
        same = across == across.T
        slot_rows.append(row)
        rank_rows.append(
            jnp.sum(jnp.where(same & (sub < lane), 1.0, 0.0), axis=0, keepdims=True).astype(
                jnp.int32
            )
        )
        rank_columns.append(
            jnp.sum(jnp.where(same & (lane < sub), 1.0, 0.0), axis=1, keepdims=True)
        )
        place = places[pl.ds(v, 1), :]
        spot = ((place & 7) * 32 + (place >> 3) + 1).astype(F32)
        place_columns.append(jnp.broadcast_to(spot, (128, 128)).T)

    lane_view, lane_rank, lane_part = (lane >> 3) & 1, (lane >> 2) & 1, lane & 3
    ids = jnp.zeros((128, 128), F32)
    for v in range(2):
        taken = jnp.where(sub == slot_rows[v], 1.0, 0.0).astype(BF16)
        mine = (lane_view == v) & (lane_rank.astype(F32) == rank_columns[v])
        ids = ids + dot(taken, jnp.where(mine, place_columns[v], 0.0).astype(BF16))
    ids = jnp.where(ids > 0.0, ids + (lane_view * 256 + lane_part * 8 - 1).astype(F32), -1.0)
    ids_out[...] = ids.reshape(128, 1, 128)

    target = jnp.concatenate(
        [
            slot_rows[v] * 16 + v * 8 + rank_rows[v] * 4 + part
            for v in range(2)
            for part in range(4)
        ],
        axis=1,
    )
    for plane in range(2):
        for v in range(2):
            for part in range(4):
                staged[plane, pl.ds((v * 4 + part) * 128, 128), :] = blocks[
                    v, :, pl.ds(plane * 1024 + part * 256, 256)
                ]
    for plane in range(2):
        pack_halo([estimate.at[plane]], True, 0, plane)

    pl.semaphore_wait(barrier, N_GX + N_GY - 2)
    for step in range(1, N_GY):
        pl.semaphore_signal(
            ready, inc=1, device_id=(gx, (gy + step) % N_GY), device_id_type=MESH
        )
    pl.semaphore_wait(ready, N_GY - 1)

    for plane in range(2):
        send_halo(0, plane)

    def id_copy(slot):
        return pltpu.make_async_remote_copy(
            src_ref=ids_out.at[pl.ds(slot, 1)],
            dst_ref=ids_in.at[pl.ds(slot, 1)],
            send_sem=ids_sent,
            recv_sem=ids_here,
            device_id=partner(slot, here),
            device_id_type=MESH,
        )

    def data_copy(plane, slot):
        rows = pl.ds(pl.multiple_of(slot * 16, 16), 16)
        return pltpu.make_async_remote_copy(
            src_ref=outgoing.at[plane, rows],
            dst_ref=incoming.at[plane, rows],
            send_sem=data_sent.at[plane],
            recv_sem=data_here.at[plane, slot // GROUP],
            device_id=partner(slot, here),
            device_id_type=MESH,
        )

    @pl.loop(1, DEVICES)
    def _(slot):
        id_copy(slot).start()

    for plane in range(2):

        @pl.loop(0, DEVICES // CHUNK)
        def _(chunk):
            rows = CHUNK * 16
            wanted = iota((rows, 1024), 0) + chunk * rows
            pick = jnp.where(wanted == target, 1.0, 0.0).astype(BF16)
            outgoing[plane, pl.ds(pl.multiple_of(chunk * rows, rows), rows), :] = dot(
                pick, staged[plane]
            ).astype(BF16)
            for j in range(CHUNK):
                slot = chunk * CHUNK + j
                if j == 0:

                    @pl.when(chunk > 0)
                    def _():
                        data_copy(plane, slot).start()

                else:
                    data_copy(plane, slot).start()

    def bands(v, plane, axis, reverse):
        kernel_index = psf_index[v, plane]
        wide = iota((8, 512), 1)
        taps = jnp.zeros((8, 512), F32)
        total = jnp.zeros((8, 512), F32)
        for t in range(TAPS):
            value = psf_taps[v, kernel_index, axis, t]
            at = 120 + (TAPS - 1 - t if reverse else t)
            taps = jnp.where(wide == at, value, taps)
            total = total + value
        return taps / total

    def natural(first):
        rows = jnp.broadcast_to(first[0:1], (TILE, 512))
        return pltpu.roll(rows, 0, 1, stride=1, stride_axis=0)

    def reordered(first):
        rows = natural(first)
        for tile in range(4):
            shuffle[tile] = rows[:, tile * 128 : (tile + 1) * 128]
        return jnp.concatenate(
            [
                jnp.concatenate(
                    [
                        shuffle[tile, pl.ds(q * 8 + x8, 8, stride=32), :]
                        for tile in range(4)
                    ],
                    axis=1,
                )
                for x8 in range(8)
                for q in range(4)
            ],
            axis=0,
        )

    has_low_x = jnp.where(gx > 0, 1.0, 0.0)
    has_high_x = jnp.where(gx < N_GX - 1, 1.0, 0.0)
    has_low_y = jnp.where(gy > 0, 1.0, 0.0)
    has_high_y = jnp.where(gy < N_GY - 1, 1.0, 0.0)

    def put(ref, index, value):
        high, low = split(value)
        ref[(0,) + index] = high
        ref[(1,) + index] = low

    lane = iota((TILE, 128), 1)
    for plane in range(2):
        back_x_side = jnp.zeros((TILE, 128), F32)
        for v in range(2):
            views = pl.ds(v * TILE, TILE)
            m = natural(bands(v, plane, 1, False))
            put(fwd_y, (plane, slice(None), views), m[:, 128:384].T)
            put(back_y, (plane, v), m[:, 128:384])
            low, high = m[:, 0:128].T[120:128] * has_low_y, m[:, 384:512].T[0:8] * has_high_y
            nothing = jnp.zeros((8, TILE), F32)
            put(
                fwd_y_halo,
                (plane, slice(None), views),
                jnp.concatenate([low, nothing, high, nothing], axis=0),
            )
            m = natural(bands(v, plane, 1, True))
            low, high = m[:, 0:128].T[120:128] * has_low_y, m[:, 384:512].T[0:8] * has_high_y
            both = [low, nothing, high, nothing] if v == 0 else [nothing, low, nothing, high]
            put(back_y_halo, (plane, v), jnp.concatenate(both, axis=0))
            m = reordered(bands(v, plane, 0, False))
            put(fwd_x, (plane, v), m[:, 128:384])
            put(back_x, (plane, v), m[:, 128:384].T)
            low = pltpu.roll(m[:, 0:128], 8, 1) * has_low_x
            high = pltpu.roll(m[:, 384:512], 16, 1) * has_high_x
            side = jnp.where(lane < 8, low, jnp.where((lane >= 16) & (lane < 24), high, 0.0))
            put(fwd_x_halo, (plane, v), side[:, :32])
            m = natural(bands(v, plane, 0, True))
            low = pltpu.roll(m[:, 0:128], 8 + 8 * v, 1) * has_low_x
            high = pltpu.roll(m[:, 384:512], 16 + 8 * v, 1) * has_high_x
            first = 8 * v
            back_x_side = jnp.where(
                (lane >= first) & (lane < first + 8),
                low,
                jnp.where((lane >= first + 16) & (lane < first + 24), high, back_x_side),
            )
        put(back_x_halo, (plane,), back_x_side[:, :32])

    def forward(field, exchange, plane):
        rows, columns = read_halo(exchange, plane)
        tall = jnp.concatenate([field.astype(BF16), rows], axis=0)
        along_y = (
            dot(tall, fwd_y[0, plane])
            + dot(tall, fwd_y[1, plane])
            + dot(columns, fwd_y_halo[0, plane])
            + dot(columns, fwd_y_halo[1, plane])
        ).astype(BF16)
        blurred = []
        for v in range(2):
            mine = along_y[:, v * TILE : (v + 1) * TILE]
            main, side = mine[:TILE], mine[TILE:]
            blurred.append(
                dot(fwd_x[0, plane, v], main)
                + dot(fwd_x[1, plane, v], main)
                + dot(fwd_x_halo[0, plane, v], side)
                + dot(fwd_x_halo[1, plane, v], side)
                + background[v, plane]
            )
        return blurred

    def correction(exchange, plane):
        rows, columns = read_halo(exchange, plane)
        total = jnp.zeros((TILE, TILE), F32)
        sides = []
        for v in range(2):
            here_ratio = jnp.concatenate([ratio[v, 0], ratio[v, 1]], axis=1)
            tall = jnp.concatenate([here_ratio.astype(BF16), rows], axis=0)
            along_y = (
                dot(tall, back_y[0, plane, v])
                + dot(tall, back_y[1, plane, v])
                + dot(columns, back_y_halo[0, plane, v])
                + dot(columns, back_y_halo[1, plane, v])
            )
            high, low = split(along_y[:TILE])
            total = (
                total
                + dot(back_x[0, plane, v], high)
                + dot(back_x[0, plane, v], low)
                + dot(back_x[1, plane, v], high)
            )
            sides.append(along_y[TILE:])
        view = (iota((32, TILE), 0) // 8) % 2
        high, low = split(jnp.where(view == 0, sides[0], sides[1]))
        return (
            total
            + dot(back_x_halo[0, plane], high)
            + dot(back_x_halo[0, plane], low)
            + dot(back_x_halo[1, plane], high)
        )

    for plane in range(2):
        wait_halo(0, plane)
        for v, blurred in enumerate(forward(estimate[plane], 0, plane)):
            inverse[plane, v] = 1.0 / blurred

    rest = ids_in.at[pl.ds(1, DEVICES - 1)]
    pltpu.make_async_copy(rest, rest, ids_here).wait()
    ids_in[pl.ds(0, 1)] = ids_out[pl.ds(0, 1)]
    spot = iota((512, 256), 0).astype(F32)
    picked = (iota((8, 128), 1) // 16) == iota((8, 128), 0)
    for group in range(GROUPS):
        halves = []
        for half in range(2):
            eight = ids_in[pl.ds(group * GROUP + half * 8, 8)].reshape(8, 128)
            halves.append(jnp.sum(jnp.where(picked, eight, 0.0), axis=0, keepdims=True))
        wanted = jnp.concatenate(halves, axis=1)
        landing[:, pl.ds(group * 256, 256)] = jnp.where(spot == wanted, 1.0, 0.0).astype(BF16)

    def land(plane):
        incoming[plane, pl.ds(0, 16)] = outgoing[plane, pl.ds(0, 16)]
        for group in range(GROUPS):
            first = group * 256
            came = (
                incoming.at[plane, pl.ds(16, 240)]
                if group == 0
                else incoming.at[plane, pl.ds(first, 256)]
            )
            pltpu.make_async_copy(came, came, data_here.at[plane, group]).wait()
            part = dot(
                landing[:, pl.ds(first, 256)], incoming[plane, pl.ds(first, 256), :]
            )
            summed[...] = part if group == 0 else summed[...] + part
        group_of = iota((32, 128), 1) // 32
        for v in range(2):
            for h in range(2):
                for wide in range(2):
                    source = [
                        summed[
                            pl.ds(v * 256 + (wide * 4 + by) * 32, 32), pl.ds(h * 128, 128)
                        ]
                        for by in range(4)
                    ]
                    for x4 in range(4):
                        tile = source[x4]
                        for by in range(4):
                            if by != x4:
                                moved = pltpu.roll(source[by], ((by - x4) % 4) * 32, 1)
                                tile = jnp.where(group_of == by, moved, tile)
                        measured[
                            v, pl.ds((h * 4 + x4) * 32, 32), pl.ds(wide * 128, 128)
                        ] = tile

    def put_ratio(v, value):
        ratio[v, 0] = value[:, :128]
        ratio[v, 1] = value[:, 128:]

    for plane in range(2):
        land(plane)
        for v in range(2):
            put_ratio(v, measured[v] * inverse[plane, v])
        pack_halo([ratio.at[0], ratio.at[1]], False, 1, plane)
        send_halo(1, plane)
        wait_halo(1, plane)
        result[plane] = estimate[plane] * (0.5 * correction(1, plane))
        pack_halo([result.at[plane]], True, 2, plane)
        send_halo(2, plane)
        wait_halo(2, plane)
        for v, blurred in enumerate(forward(result[plane], 2, plane)):
            put_ratio(v, measured[v] / blurred)
        pack_halo([ratio.at[0], ratio.at[1]], False, 3, plane)
        send_halo(3, plane)
        wait_halo(3, plane)
        result[plane] = result[plane] * (0.5 * correction(3, plane))

    rest = ids_out.at[pl.ds(1, DEVICES - 1)]
    pltpu.make_async_copy(rest, rest, ids_sent).wait()
    for plane in range(2):
        rest = outgoing.at[plane, pl.ds(16, (DEVICES - 1) * 16)]
        pltpu.make_async_copy(rest, rest, data_sent.at[plane]).wait()
        for exchange in range(4):
            whole = halo_out.at[exchange, plane]
            pltpu.make_async_copy(whole, whole, halo_sent.at[exchange, plane]).wait()


def shards(blocks, owner_route, block_slot, estimate, background, psf_taps, psf_index):
    owners = owner_route.reshape(owner_route.shape[:2])
    vmem = pl.BlockSpec(memory_space=pltpu.VMEM)
    smem = pl.BlockSpec(memory_space=pltpu.SMEM)
    dma = pltpu.SemaphoreType.DMA
    return pl.pallas_call(
        kernel,
        out_shape=jax.ShapeDtypeStruct(estimate.shape, F32),
        in_specs=[vmem, vmem, vmem, vmem, smem, smem, smem],
        out_specs=vmem,
        scratch_shapes=[
            pltpu.VMEM((2, 1024, 256), BF16),
            pltpu.VMEM((2, DEVICES * 16, 256), BF16),
            pltpu.VMEM((2, DEVICES * 16, 256), BF16),
            pltpu.VMEM((DEVICES, 1, 128), F32),
            pltpu.VMEM((DEVICES, 1, 128), F32),
            pltpu.VMEM((512, DEVICES * 16), BF16),
            pltpu.VMEM((512, 256), F32),
            pltpu.VMEM((2, TILE, TILE), F32),
            pltpu.VMEM((2, 2, TILE, TILE), F32),
            pltpu.VMEM((2, 2, TILE, 128), F32),
            pltpu.VMEM((4, TILE, 128), F32),
            pltpu.VMEM((4, 2, HALO_ROWS, 128), BF16),
            pltpu.VMEM((4, 2, HALO_ROWS, 128), BF16),
            pltpu.VMEM((2, 2, TILE, 2 * TILE), BF16),
            pltpu.VMEM((2, 2, 32, 2 * TILE), BF16),
            pltpu.VMEM((2, 2, 2, TILE, TILE), BF16),
            pltpu.VMEM((2, 2, 2, TILE, 32), BF16),
            pltpu.VMEM((2, 2, 2, TILE, TILE), BF16),
            pltpu.VMEM((2, 2, 2, 32, TILE), BF16),
            pltpu.VMEM((2, 2, 2, TILE, TILE), BF16),
            pltpu.VMEM((2, 2, TILE, 32), BF16),
            pltpu.SemaphoreType.REGULAR,
            dma((2,)),
            dma((2, GROUPS)),
            dma,
            dma,
            dma((4, 2)),
            dma((4, 2)),
        ],
        compiler_params=pltpu.CompilerParams(
            collective_id=0, has_side_effects=True, vmem_limit_bytes=48 << 20
        ),
        cost_estimate=pl.CostEstimate(
            flops=8_000_000_000, bytes_accessed=2 << 20, transcendentals=0
        ),
    )(blocks, owners, block_slot, estimate, background, psf_taps, psf_index)


def solution(mesh):
    return jax.shard_map(
        shards,
        mesh=mesh,
        in_specs=(
            P(None, ("gx", "gy"), None),
            P(None, ("gx", "gy"), None),
            P(None, ("gx", "gy")),
            P(None, "gx", "gy"),
            P(),
            P(),
            P(),
        ),
        out_specs=P(None, "gx", "gy"),
        check_vma=False,
    )
```

```python
import jax
import jax.numpy as jnp
from jax import lax
from jax.experimental import pallas as pl
from jax.experimental.pallas import tpu as pltpu
from jax.sharding import PartitionSpec as P

MESH = pl.DeviceIdType.MESH
F32 = jnp.float32
BF16 = jnp.bfloat16

N_GX, N_GY = 16, 8
DEVICES = N_GX * N_GY
TILE = 256
TAPS = 17
WIDE = TILE + 64
LANES = 384
STEP, STEP_INVERSE = 27, 19
GROUP = 16
GROUPS = DEVICES // GROUP
EARLY = 2
ESTIMATE_PARTS = (
    (0, 64, 1, 0),
    (64, 64, -1, 0),
    (128, 64, 0, 1),
    (192, 64, 0, -1),
    (256, 32, 1, 1),
    (288, 32, 1, -1),
    (320, 32, -1, 1),
    (352, 32, -1, -1),
)
ESTIMATE_ROWS = 384
SIDE_PARTS = ((256, 128, 0, 1), (384, 128, 0, -1))
OTHER_PARTS = (
    (0, 128, 1, 0),
    (128, 128, -1, 0),
    (512, 32, 1, 1),
    (544, 32, 1, -1),
    (576, 32, -1, 1),
    (608, 32, -1, -1),
)
MEASURED_ROWS = 640


def iota(shape, dim):
    return lax.broadcasted_iota(jnp.int32, shape, dim)


def dot(a, b):
    return jnp.dot(a, b, preferred_element_type=F32)


def split(a):
    high = a.astype(BF16)
    return high, (a - high.astype(F32)).astype(BF16)


def torus_position():
    gx, gy = lax.axis_index("gx"), lax.axis_index("gy")
    return gy // 2, ((gx // 2) % 2) * 2 + gy % 2, gx // 4, gx % 2


def partner(slot, here):
    x, y, z, core = here
    shift = (slot * STEP) % DEVICES
    core = (core + shift % 2) % 2
    x = (x + (shift // 2) % 4) % 4
    y = (y + (shift // 8) % 4) % 4
    z = (z + shift // 32) % 4
    return z * 4 + (y // 2) * 2 + core, x * 2 + y % 2


def slot_of(tile, here):
    x, y, z, core = here
    gx, gy = tile >> 3, tile & 7
    d_core = ((gx & 1) - core) & 1
    dx = ((gy >> 1) - x) & 3
    dy = ((((gx >> 1) & 1) * 2 + (gy & 1)) - y) & 3
    dz = ((gx >> 2) - z) & 3
    return ((d_core + 2 * dx + 8 * dy + 32 * dz) * STEP_INVERSE) & (DEVICES - 1)


def kernel(
    blocks_in,
    owners_in,
    places_in,
    estimate_in,
    background_in,
    taps_in,
    index_in,
    result,
    blocks,
    owners,
    places,
    estimate,
    background,
    psf_taps,
    psf_index,
    staged,
    outgoing,
    incoming,
    ids_out,
    ids_in,
    landing,
    summed,
    wide_estimate,
    measured,
    inverse,
    final,
    shuffle,
    estimate_out,
    estimate_halo,
    measured_out,
    measured_halo,
    fwd_y,
    fwd_x,
    back_y,
    back_x,
    ready,
    loaded,
    stored,
    data_sent,
    data_here,
    ids_sent,
    ids_here,
    estimate_sent,
    estimate_here,
    measured_sent,
    measured_here,
):
    gx, gy = lax.axis_index("gx"), lax.axis_index("gy")
    here = torus_position()
    barrier = pltpu.get_barrier_semaphore()

    loads = [
        pltpu.make_async_copy(source, target, loaded.at[i])
        for i, (source, target) in enumerate(
            (
                (owners_in, owners),
                (places_in, places),
                (estimate_in, estimate),
                (blocks_in, blocks),
                (background_in, background),
                (taps_in, psf_taps),
                (index_in, psf_index),
            )
        )
    ]
    for load in loads:
        load.start()

    for step in range(1, N_GX):
        pl.semaphore_signal(
            barrier, inc=1, device_id=((gx + step) % N_GX, gy), device_id_type=MESH
        )
    for step in range(1, N_GY):
        pl.semaphore_signal(
            barrier, inc=1, device_id=(gx, (gy + step) % N_GY), device_id_type=MESH
        )

    has_low_x = jnp.where(gx > 0, 1.0, 0.0)
    has_high_x = jnp.where(gx < N_GX - 1, 1.0, 0.0)
    has_low_y = jnp.where(gy > 0, 1.0, 0.0)
    has_high_y = jnp.where(gy < N_GY - 1, 1.0, 0.0)
    narrow = iota((32, 128), 1)

    def turn(a, shift):
        return pltpu.roll(a, shift % 128, 1) if shift % 128 else a

    def sides(low, high):
        at = iota(low.shape, 1)
        return jnp.where(
            at < 32, low * has_low_y, jnp.where(at < 64, high * has_high_y, 0.0)
        )

    def send_parts(parts, out, into, sent, arrived):
        for start, rows, to_x, to_y in parts:
            pltpu.make_async_remote_copy(
                src_ref=out.at[pl.ds(start, rows)],
                dst_ref=into.at[pl.ds(start, rows)],
                send_sem=sent,
                recv_sem=arrived,
                device_id=((gx + to_x + N_GX) % N_GX, (gy + to_y + N_GY) % N_GY),
                device_id_type=MESH,
            ).start()

    def pack_estimate(plane):
        out = estimate_out.at[plane]
        for at, row in ((0, 224), (64, 0)):
            for tile in range(2):
                out[pl.ds(at + 32 * tile, 32)] = estimate[
                    plane, pl.ds(row, 32), pl.ds(128 * tile, 128)
                ].astype(BF16)
        for at, tile in ((128, 1), (192, 0)):
            packed = jnp.zeros((64, 128), F32)
            for slab in range(4):
                piece = estimate[plane, pl.ds(64 * slab, 64), pl.ds(128 * tile, 128)]
                moved = turn(piece, 32 * slab + 32 * tile)
                packed = jnp.where(iota((64, 128), 1) // 32 == slab, moved, packed)
            out[pl.ds(at, 64)] = packed.astype(BF16)
        for at, row, tile in ((256, 224, 1), (288, 224, 0), (320, 0, 1), (352, 0, 0)):
            out[pl.ds(at, 32)] = estimate[
                plane, pl.ds(row, 32), pl.ds(128 * tile, 128)
            ].astype(BF16)

    def widen_estimate(plane):
        whole = estimate_halo.at[plane]
        pltpu.make_async_copy(whole, whole, estimate_here.at[plane]).wait()

        def got(start, rows):
            return estimate_halo[plane, pl.ds(start, rows)].astype(F32)

        wide = wide_estimate.at[plane]
        wide[pl.ds(0, TILE), pl.ds(0, TILE)] = estimate[plane]
        for slab in range(4):
            wide[pl.ds(64 * slab, 64), pl.ds(TILE, 128)] = sides(
                turn(got(128, 64), -32 * slab), turn(got(192, 64), 32 - 32 * slab)
            )
        for row, start, corner, there in (
            (TILE, 0, 256, has_low_x),
            (TILE + 32, 64, 320, has_high_x),
        ):
            for tile in range(2):
                wide[pl.ds(row, 32), pl.ds(128 * tile, 128)] = (
                    got(start + 32 * tile, 32) * there
                )
            wide[pl.ds(row, 32), pl.ds(TILE, 128)] = (
                sides(turn(got(corner, 32), 32), turn(got(corner + 32, 32), 32)) * there
            )

    def send_sides(plane):
        for at, by in ((256, 7), (384, 0)):
            for v in range(2):
                for h in range(2):
                    measured_out[plane, pl.ds(at + 64 * v + 32 * h, 32)] = summed[
                        pl.ds(v * 256 + by * 32, 32), pl.ds(128 * h, 128)
                    ].astype(BF16)
        send_parts(
            SIDE_PARTS,
            measured_out.at[plane],
            measured_halo.at[plane],
            measured_sent.at[plane],
            measured_here.at[plane],
        )

    def send_others(plane):
        out = measured_out.at[plane]

        def edge(v, tile, bx):
            return jnp.concatenate(
                [measured[v, tile, pl.ds(q * 8 + bx, 8, stride=32), :] for q in range(4)], axis=0
            )

        for at, bx, corner in ((0, 7, 512), (128, 0, 576)):
            for tile in range(2):
                edges = [edge(v, tile, bx) for v in range(2)]
                for v in range(2):
                    out[pl.ds(at + 64 * v + 32 * tile, 32)] = edges[v].astype(BF16)
                if tile == 1:
                    both = jnp.where(narrow >= 96, edges[0], turn(edges[1], 96))
                    out[pl.ds(corner, 32)] = both.astype(BF16)
                else:
                    both = jnp.where(narrow < 32, edges[0], turn(edges[1], 32))
                    out[pl.ds(corner + 32, 32)] = both.astype(BF16)
        send_parts(
            OTHER_PARTS,
            measured_out.at[plane],
            measured_halo.at[plane],
            measured_sent.at[plane],
            measured_here.at[plane],
        )

    def widen_measured(plane):
        whole = measured_halo.at[plane]
        pltpu.make_async_copy(whole, whole, measured_here.at[plane]).wait()

        def got(start):
            return measured_halo[plane, pl.ds(start, 32)].astype(F32)

        for v in range(2):
            for x8 in range(8):
                at, back = 64 * v + 32 * (x8 // 4), -32 * (x8 % 4)
                measured[v, 2, pl.ds(32 * x8, 32), :] = sides(
                    turn(got(256 + at), back), turn(got(384 + at), back + 32)
                )
            for row, start, corner, there in (
                (TILE, 0, 512, has_low_x),
                (TILE + 32, 128, 576, has_high_x),
            ):
                for tile in range(2):
                    measured[v, tile, pl.ds(row, 32), :] = (
                        got(start + 64 * v + 32 * tile) * there
                    )
                measured[v, 2, pl.ds(row, 32), :] = (
                    sides(
                        turn(got(corner), 32 + 32 * v), turn(got(corner + 32), 32 - 32 * v)
                    )
                    * there
                )

    loads[0].wait()
    loads[1].wait()
    slot_rows, rank_rows, rank_columns, place_columns = [], [], [], []
    sub, lane = iota((128, 128), 0), iota((128, 128), 1)
    for v in range(2):
        row = slot_of(owners[pl.ds(v, 1), :], here)
        across = jnp.broadcast_to(row, (128, 128))
        same = across == across.T
        slot_rows.append(row)
        rank_rows.append(
            jnp.sum(jnp.where(same & (sub < lane), 1.0, 0.0), axis=0, keepdims=True).astype(
                jnp.int32
            )
        )
        rank_columns.append(
            jnp.sum(jnp.where(same & (lane < sub), 1.0, 0.0), axis=1, keepdims=True)
        )
        place = places[pl.ds(v, 1), :]
        spot = ((place & 7) * 32 + (place >> 3) + 1).astype(F32)
        place_columns.append(jnp.broadcast_to(spot, (128, 128)).T)

    lane_view, lane_rank, lane_part = (lane >> 3) & 1, (lane >> 2) & 1, lane & 3
    ids = jnp.zeros((128, 128), F32)
    for v in range(2):
        taken = jnp.where(sub == slot_rows[v], 1.0, 0.0).astype(BF16)
        mine = (lane_view == v) & (lane_rank.astype(F32) == rank_columns[v])
        ids = ids + dot(taken, jnp.where(mine, place_columns[v], 0.0).astype(BF16))
    ids = jnp.where(ids > 0.0, ids + (lane_view * 256 + lane_part * 8 - 1).astype(F32), -1.0)
    ids_out[...] = ids.reshape(128, 1, 128)

    target = jnp.concatenate(
        [
            slot_rows[v] * 16 + v * 8 + rank_rows[v] * 4 + part
            for v in range(2)
            for part in range(4)
        ],
        axis=1,
    )
    loads[3].wait()
    for plane in range(2):
        for v in range(2):
            for part in range(4):
                staged[plane, pl.ds((v * 4 + part) * 128, 128), :] = blocks[
                    v, :, pl.ds(plane * 1024 + part * 256, 256)
                ]
    loads[2].wait()
    for plane in range(2):
        pack_estimate(plane)

    pl.semaphore_wait(barrier, N_GX + N_GY - 2)
    for step in range(1, N_GY):
        pl.semaphore_signal(
            ready, inc=1, device_id=(gx, (gy + step) % N_GY), device_id_type=MESH
        )
    pl.semaphore_wait(ready, N_GY - 1)

    for plane in range(2):
        send_parts(
            ESTIMATE_PARTS,
            estimate_out.at[plane],
            estimate_halo.at[plane],
            estimate_sent.at[plane],
            estimate_here.at[plane],
        )

    def id_copy(slot):
        return pltpu.make_async_remote_copy(
            src_ref=ids_out.at[pl.ds(slot, 1)],
            dst_ref=ids_in.at[pl.ds(slot, 1)],
            send_sem=ids_sent,
            recv_sem=ids_here,
            device_id=partner(slot, here),
            device_id_type=MESH,
        )

    def data_copy(plane, slot):
        rows = pl.ds(pl.multiple_of(slot * 16, 16), 16)
        return pltpu.make_async_remote_copy(
            src_ref=outgoing.at[plane, rows],
            dst_ref=incoming.at[plane, rows],
            send_sem=data_sent.at[plane],
            recv_sem=data_here.at[plane, slot // GROUP],
            device_id=partner(slot, here),
            device_id_type=MESH,
        )

    @pl.loop(1, DEVICES)
    def _(slot):
        id_copy(slot).start()

    def pick_group(plane, group):
        rows = GROUP * 16
        wanted = iota((rows, 1024), 0) + group * rows
        pick = jnp.where(wanted == target, 1.0, 0.0).astype(BF16)
        outgoing[plane, pl.ds(pl.multiple_of(group * rows, rows), rows), :] = dot(
            pick, staged[plane]
        ).astype(BF16)

    def send_group(plane, group):
        for j in range(GROUP):
            if j == 0:

                @pl.when(group > 0)
                def _():
                    data_copy(plane, group * GROUP).start()

            else:
                data_copy(plane, group * GROUP + j).start()

    @pl.loop(0, GROUPS)
    def _(group):
        pick_group(0, group)
        send_group(0, group)

    @pl.loop(0, GROUPS)
    def _(group):
        pick_group(1, group)

        @pl.when(group < EARLY)
        def _():
            send_group(1, group)

    for load in loads[4:]:
        load.wait()

    def bands(v, plane, axis, reverse):
        kernel_index = psf_index[v, plane]
        wide = iota((8, 512), 1)
        taps = jnp.zeros((8, 512), F32)
        total = jnp.zeros((8, 512), F32)
        for t in range(TAPS):
            value = psf_taps[v, kernel_index, axis, t]
            at = 88 + (TAPS - 1 - t if reverse else t)
            taps = jnp.where(wide == at, value, taps)
            total = total + value
        rows = jnp.broadcast_to((taps / total)[0:1], (WIDE, 512))
        return pltpu.roll(rows, 0, 1, stride=1, stride_axis=0)

    def by_lanes(m):
        at = iota((m.shape[0], 128), 1)
        side = jnp.where(
            at < 32, turn(m[:, :128], 32), jnp.where(at < 64, turn(m[:, 384:], 32), 0.0)
        )
        return jnp.concatenate([m[:, 128:384], side], axis=1)

    def by_rows(m):
        return jnp.concatenate([m[32 : 32 + TILE], m[:32], m[32 + TILE :]], axis=0)

    def reordered(m):
        for tile in range(4):
            shuffle[tile] = m[:, tile * 128 : (tile + 1) * 128]
        main = [
            jnp.concatenate(
                [
                    shuffle[tile, pl.ds(32 + q * 8 + x8, 8, stride=32), :]
                    for tile in range(4)
                ],
                axis=1,
            )
            for x8 in range(8)
            for q in range(4)
        ]
        return jnp.concatenate(main + [m[:32], m[32 + TILE :]], axis=0)

    def put(ref, index, value):
        high, low = split(value)
        ref[(0,) + index] = high
        ref[(1,) + index] = low

    for plane in range(2):
        for v in range(2):
            m = by_lanes(by_rows(bands(v, plane, 1, True)))
            put(fwd_y, (plane, slice(None), pl.ds(v * LANES, LANES)), m)
            put(back_y, (plane, v), by_lanes(by_rows(bands(v, plane, 1, False))))
            m = by_lanes(reordered(bands(v, plane, 0, False)))
            put(fwd_x, (plane, v), m[:, :WIDE])
            square = jnp.concatenate([m, jnp.zeros((LANES - WIDE, LANES), F32)], axis=0)
            put(back_x, (plane, v), square.T[:WIDE, :WIDE])

    def forward(field, plane):
        field = field.astype(BF16)[:, :WIDE]
        along_y = (dot(field, fwd_y[0, plane]) + dot(field, fwd_y[1, plane])).astype(BF16)
        blurred = []
        for v in range(2):
            mine = along_y[:, v * LANES : (v + 1) * LANES]
            blurred.append(
                dot(fwd_x[0, plane, v], mine)
                + dot(fwd_x[1, plane, v], mine)
                + background[v, plane]
            )
        return blurred

    def correction(ratios, plane, rows, lanes):
        total = jnp.zeros((rows, lanes), F32)
        for v in range(2):
            ratio = ratios[v].astype(BF16)[:, :WIDE]
            high, low = split(
                dot(ratio, back_y[0, plane, v][:, :lanes])
                + dot(ratio, back_y[1, plane, v][:, :lanes])
            )
            total = (
                total
                + dot(back_x[0, plane, v][:rows], high)
                + dot(back_x[0, plane, v][:rows], low)
                + dot(back_x[1, plane, v][:rows], high)
            )
        return total

    for plane in range(2):
        widen_estimate(plane)
        for v, blurred in enumerate(forward(wide_estimate[plane], plane)):
            inverse[plane, v] = 1.0 / blurred

    rest = ids_in.at[pl.ds(1, DEVICES - 1)]
    pltpu.make_async_copy(rest, rest, ids_here).wait()
    ids_in[pl.ds(0, 1)] = ids_out[pl.ds(0, 1)]
    spot = iota((512, 256), 0).astype(F32)
    picked = (iota((8, 128), 1) // 16) == iota((8, 128), 0)
    for group in range(GROUPS):
        halves = []
        for half in range(2):
            eight = ids_in[pl.ds(group * GROUP + half * 8, 8)].reshape(8, 128)
            halves.append(jnp.sum(jnp.where(picked, eight, 0.0), axis=0, keepdims=True))
        wanted = jnp.concatenate(halves, axis=1)
        landing[:, pl.ds(group * 256, 256)] = jnp.where(spot == wanted, 1.0, 0.0).astype(BF16)

    def land(plane):
        incoming[plane, pl.ds(0, 16)] = outgoing[plane, pl.ds(0, 16)]
        for group in range(GROUPS):
            first = group * 256
            came = (
                incoming.at[plane, pl.ds(16, 240)]
                if group == 0
                else incoming.at[plane, pl.ds(first, 256)]
            )
            pltpu.make_async_copy(came, came, data_here.at[plane, group]).wait()
            part = dot(
                landing[:, pl.ds(first, 256)], incoming[plane, pl.ds(first, 256), :]
            )
            summed[...] = part if group == 0 else summed[...] + part
        send_sides(plane)
        group_of = narrow // 32
        for v in range(2):
            for h in range(2):
                for wide in range(2):
                    source = [
                        summed[
                            pl.ds(v * 256 + (wide * 4 + by) * 32, 32), pl.ds(h * 128, 128)
                        ]
                        for by in range(4)
                    ]
                    for x4 in range(4):
                        tile = source[x4]
                        for by in range(4):
                            if by != x4:
                                moved = pltpu.roll(source[by], ((by - x4) % 4) * 32, 1)
                                tile = jnp.where(group_of == by, moved, tile)
                        measured[v, wide, pl.ds((h * 4 + x4) * 32, 32), :] = tile

    def wide_measured(v):
        return jnp.concatenate([measured[v, tile] for tile in range(3)], axis=1)

    def store(plane):
        return pltpu.make_async_copy(final.at[plane], result.at[plane], stored.at[plane])

    for plane in range(2):
        land(plane)
        send_others(plane)
        if plane == 0:

            @pl.loop(EARLY, GROUPS)
            def _(group):
                send_group(1, group)

        widen_measured(plane)
        ratios = [wide_measured(v) * inverse[plane, v] for v in range(2)]
        current = wide_estimate[plane] * (0.5 * correction(ratios, plane, WIDE, LANES))
        ratios = [
            wide_measured(v) / blurred for v, blurred in enumerate(forward(current, plane))
        ]
        final[plane] = current[:TILE, :TILE] * (
            0.5 * correction(ratios, plane, TILE, TILE)
        )
        store(plane).start()

    rest = ids_out.at[pl.ds(1, DEVICES - 1)]
    pltpu.make_async_copy(rest, rest, ids_sent).wait()
    for plane in range(2):
        rest = outgoing.at[plane, pl.ds(16, (DEVICES - 1) * 16)]
        pltpu.make_async_copy(rest, rest, data_sent.at[plane]).wait()
        whole = estimate_out.at[plane]
        pltpu.make_async_copy(whole, whole, estimate_sent.at[plane]).wait()
        whole = measured_out.at[plane]
        pltpu.make_async_copy(whole, whole, measured_sent.at[plane]).wait()
        store(plane).wait()


def shards(blocks, owner_route, block_slot, estimate, background, psf_taps, psf_index):
    owners = owner_route.reshape(owner_route.shape[:2])
    anywhere = pl.BlockSpec(memory_space=pl.ANY)
    dma = pltpu.SemaphoreType.DMA
    return pl.pallas_call(
        kernel,
        out_shape=jax.ShapeDtypeStruct(estimate.shape, F32),
        in_specs=[anywhere] * 7,
        out_specs=anywhere,
        scratch_shapes=[
            pltpu.VMEM(blocks.shape, BF16),
            pltpu.VMEM(owners.shape, jnp.int32),
            pltpu.VMEM(block_slot.shape, jnp.int32),
            pltpu.VMEM(estimate.shape, F32),
            pltpu.SMEM(background.shape, F32),
            pltpu.SMEM(psf_taps.shape, F32),
            pltpu.SMEM(psf_index.shape, jnp.int32),
            pltpu.VMEM((2, 1024, 256), BF16),
            pltpu.VMEM((2, DEVICES * 16, 256), BF16),
            pltpu.VMEM((2, DEVICES * 16, 256), BF16),
            pltpu.VMEM((DEVICES, 1, 128), F32),
            pltpu.VMEM((DEVICES, 1, 128), F32),
            pltpu.VMEM((512, DEVICES * 16), BF16),
            pltpu.VMEM((512, 256), F32),
            pltpu.VMEM((2, WIDE, LANES), F32),
            pltpu.VMEM((2, 3, WIDE, 128), F32),
            pltpu.VMEM((2, 2, WIDE, LANES), F32),
            pltpu.VMEM((2, TILE, TILE), F32),
            pltpu.VMEM((4, WIDE, 128), F32),
            pltpu.VMEM((2, ESTIMATE_ROWS, 128), BF16),
            pltpu.VMEM((2, ESTIMATE_ROWS, 128), BF16),
            pltpu.VMEM((2, MEASURED_ROWS, 128), BF16),
            pltpu.VMEM((2, MEASURED_ROWS, 128), BF16),
            pltpu.VMEM((2, 2, WIDE, 2 * LANES), BF16),
            pltpu.VMEM((2, 2, 2, WIDE, WIDE), BF16),
            pltpu.VMEM((2, 2, 2, WIDE, LANES), BF16),
            pltpu.VMEM((2, 2, 2, WIDE, WIDE), BF16),
            pltpu.SemaphoreType.REGULAR,
            dma((7,)),
            dma((2,)),
            dma((2,)),
            dma((2, GROUPS)),
            dma,
            dma,
            dma((2,)),
            dma((2,)),
            dma((2,)),
            dma((2,)),
        ],
        compiler_params=pltpu.CompilerParams(
            collective_id=0, has_side_effects=True, vmem_limit_bytes=48 << 20
        ),
        cost_estimate=pl.CostEstimate(
            flops=8_000_000_000, bytes_accessed=2 << 20, transcendentals=0
        ),
    )(blocks, owners, block_slot, estimate, background, psf_taps, psf_index)


def solution(mesh):
    return jax.shard_map(
        shards,
        mesh=mesh,
        in_specs=(
            P(None, ("gx", "gy"), None),
            P(None, ("gx", "gy"), None),
            P(None, ("gx", "gy")),
            P(None, "gx", "gy"),
            P(),
            P(),
            P(),
        ),
        out_specs=P(None, "gx", "gy"),
        check_vma=False,
    )
```

```python
import jax
import jax.numpy as jnp
from jax import lax
from jax.experimental import pallas as pl
from jax.experimental.pallas import tpu as pltpu
from jax.sharding import PartitionSpec as P

MESH = pl.DeviceIdType.MESH
F32 = jnp.float32
BF16 = jnp.bfloat16

N_GX, N_GY = 16, 8
DEVICES = N_GX * N_GY
TILE = 256
TAPS = 17
WIDE = TILE + 64
LANES = 384
STEP, STEP_INVERSE = 27, 19
GROUP = 16
GROUPS = DEVICES // GROUP
ESTIMATE_PARTS = (
    (0, 64, 1, 0),
    (64, 64, -1, 0),
    (128, 64, 0, 1),
    (192, 64, 0, -1),
    (256, 32, 1, 1),
    (288, 32, 1, -1),
    (320, 32, -1, 1),
    (352, 32, -1, -1),
)
ESTIMATE_ROWS = 384
SIDE_PARTS = ((256, 128, 0, 1), (384, 128, 0, -1))
OTHER_PARTS = (
    (0, 128, 1, 0),
    (128, 128, -1, 0),
    (512, 32, 1, 1),
    (544, 32, 1, -1),
    (576, 32, -1, 1),
    (608, 32, -1, -1),
)
MEASURED_ROWS = 640


def iota(shape, dim):
    return lax.broadcasted_iota(jnp.int32, shape, dim)


def dot(a, b):
    return jnp.dot(a, b, preferred_element_type=F32)


def split(a):
    high = a.astype(BF16)
    return high, (a - high.astype(F32)).astype(BF16)


def torus_position():
    gx, gy = lax.axis_index("gx"), lax.axis_index("gy")
    return gy // 2, ((gx // 2) % 2) * 2 + gy % 2, gx // 4, gx % 2


def partner(slot, here):
    x, y, z, core = here
    shift = (slot * STEP) % DEVICES
    core = (core + shift % 2) % 2
    x = (x + (shift // 2) % 4) % 4
    y = (y + (shift // 8) % 4) % 4
    z = (z + shift // 32) % 4
    return z * 4 + (y // 2) * 2 + core, x * 2 + y % 2


def slot_of(tile, here):
    x, y, z, core = here
    gx, gy = tile >> 3, tile & 7
    d_core = ((gx & 1) - core) & 1
    dx = ((gy >> 1) - x) & 3
    dy = ((((gx >> 1) & 1) * 2 + (gy & 1)) - y) & 3
    dz = ((gx >> 2) - z) & 3
    return ((d_core + 2 * dx + 8 * dy + 32 * dz) * STEP_INVERSE) & (DEVICES - 1)


def kernel(
    blocks_in,
    owners_in,
    places_in,
    estimate_in,
    background_in,
    taps_in,
    index_in,
    result,
    blocks,
    owners,
    places,
    estimate,
    background,
    psf_taps,
    psf_index,
    staged,
    outgoing,
    incoming,
    ids_out,
    ids_in,
    landing,
    summed,
    wide_estimate,
    measured,
    inverse,
    shuffle,
    estimate_out,
    estimate_halo,
    measured_out,
    measured_halo,
    fwd_y,
    fwd_x,
    back_y,
    back_x,
    ready,
    loaded,
    data_sent,
    data_here,
    ids_sent,
    ids_here,
    estimate_sent,
    estimate_here,
    measured_sent,
    measured_here,
):
    gx, gy = lax.axis_index("gx"), lax.axis_index("gy")
    here = torus_position()
    barrier = pltpu.get_barrier_semaphore()

    loads = [
        pltpu.make_async_copy(source, target, loaded.at[i])
        for i, (source, target) in enumerate(
            (
                (owners_in, owners),
                (places_in, places),
                (estimate_in, estimate),
                (blocks_in, blocks),
                (background_in, background),
                (taps_in, psf_taps),
                (index_in, psf_index),
            )
        )
    ]
    for load in loads:
        load.start()

    for step in range(1, N_GX):
        pl.semaphore_signal(
            barrier, inc=1, device_id=((gx + step) % N_GX, gy), device_id_type=MESH
        )
    for step in range(1, N_GY):
        pl.semaphore_signal(
            barrier, inc=1, device_id=(gx, (gy + step) % N_GY), device_id_type=MESH
        )

    has_low_x = jnp.where(gx > 0, 1.0, 0.0)
    has_high_x = jnp.where(gx < N_GX - 1, 1.0, 0.0)
    has_low_y = jnp.where(gy > 0, 1.0, 0.0)
    has_high_y = jnp.where(gy < N_GY - 1, 1.0, 0.0)
    narrow = iota((32, 128), 1)

    def turn(a, shift):
        return pltpu.roll(a, shift % 128, 1) if shift % 128 else a

    def sides(low, high):
        at = iota(low.shape, 1)
        return jnp.where(
            at < 32, low * has_low_y, jnp.where(at < 64, high * has_high_y, 0.0)
        )

    def send_parts(parts, out, into, sent, arrived):
        for start, rows, to_x, to_y in parts:
            pltpu.make_async_remote_copy(
                src_ref=out.at[pl.ds(start, rows)],
                dst_ref=into.at[pl.ds(start, rows)],
                send_sem=sent,
                recv_sem=arrived,
                device_id=((gx + to_x + N_GX) % N_GX, (gy + to_y + N_GY) % N_GY),
                device_id_type=MESH,
            ).start()

    def pack_estimate(plane):
        out = estimate_out.at[plane]
        for at, row in ((0, 224), (64, 0)):
            for tile in range(2):
                out[pl.ds(at + 32 * tile, 32)] = estimate[
                    plane, pl.ds(row, 32), pl.ds(128 * tile, 128)
                ].astype(BF16)
        for at, tile in ((128, 1), (192, 0)):
            packed = jnp.zeros((64, 128), F32)
            for slab in range(4):
                piece = estimate[plane, pl.ds(64 * slab, 64), pl.ds(128 * tile, 128)]
                moved = turn(piece, 32 * slab + 32 * tile)
                packed = jnp.where(iota((64, 128), 1) // 32 == slab, moved, packed)
            out[pl.ds(at, 64)] = packed.astype(BF16)
        for at, row, tile in ((256, 224, 1), (288, 224, 0), (320, 0, 1), (352, 0, 0)):
            out[pl.ds(at, 32)] = estimate[
                plane, pl.ds(row, 32), pl.ds(128 * tile, 128)
            ].astype(BF16)

    def widen_estimate(plane):
        whole = estimate_halo.at[plane]
        pltpu.make_async_copy(whole, whole, estimate_here.at[plane]).wait()

        def got(start, rows):
            return estimate_halo[plane, pl.ds(start, rows)].astype(F32)

        wide = wide_estimate.at[plane]
        wide[pl.ds(0, TILE), pl.ds(0, TILE)] = estimate[plane]
        for slab in range(4):
            wide[pl.ds(64 * slab, 64), pl.ds(TILE, 128)] = sides(
                turn(got(128, 64), -32 * slab), turn(got(192, 64), 32 - 32 * slab)
            )
        for row, start, corner, there in (
            (TILE, 0, 256, has_low_x),
            (TILE + 32, 64, 320, has_high_x),
        ):
            for tile in range(2):
                wide[pl.ds(row, 32), pl.ds(128 * tile, 128)] = (
                    got(start + 32 * tile, 32) * there
                )
            wide[pl.ds(row, 32), pl.ds(TILE, 128)] = (
                sides(turn(got(corner, 32), 32), turn(got(corner + 32, 32), 32)) * there
            )

    def send_sides(plane):
        for at, by in ((256, 7), (384, 0)):
            for v in range(2):
                for h in range(2):
                    measured_out[plane, pl.ds(at + 64 * v + 32 * h, 32)] = summed[
                        pl.ds(v * 256 + by * 32, 32), pl.ds(128 * h, 128)
                    ].astype(BF16)
        send_parts(
            SIDE_PARTS,
            measured_out.at[plane],
            measured_halo.at[plane],
            measured_sent.at[plane],
            measured_here.at[plane],
        )

    def send_others(plane):
        out = measured_out.at[plane]

        def edge(v, tile, bx):
            return jnp.concatenate(
                [measured[plane, v, tile, pl.ds(q * 8 + bx, 8, stride=32), :] for q in range(4)], axis=0
            )

        for at, bx, corner in ((0, 7, 512), (128, 0, 576)):
            for tile in range(2):
                edges = [edge(v, tile, bx) for v in range(2)]
                for v in range(2):
                    out[pl.ds(at + 64 * v + 32 * tile, 32)] = edges[v].astype(BF16)
                if tile == 1:
                    both = jnp.where(narrow >= 96, edges[0], turn(edges[1], 96))
                    out[pl.ds(corner, 32)] = both.astype(BF16)
                else:
                    both = jnp.where(narrow < 32, edges[0], turn(edges[1], 32))
                    out[pl.ds(corner + 32, 32)] = both.astype(BF16)
        send_parts(
            OTHER_PARTS,
            measured_out.at[plane],
            measured_halo.at[plane],
            measured_sent.at[plane],
            measured_here.at[plane],
        )

    def widen_measured(plane):
        whole = measured_halo.at[plane]
        pltpu.make_async_copy(whole, whole, measured_here.at[plane]).wait()

        def got(start):
            return measured_halo[plane, pl.ds(start, 32)].astype(F32)

        for v in range(2):
            for x8 in range(8):
                at, back = 64 * v + 32 * (x8 // 4), -32 * (x8 % 4)
                measured[plane, v, 2, pl.ds(32 * x8, 32), :] = sides(
                    turn(got(256 + at), back), turn(got(384 + at), back + 32)
                )
            for row, start, corner, there in (
                (TILE, 0, 512, has_low_x),
                (TILE + 32, 128, 576, has_high_x),
            ):
                for tile in range(2):
                    measured[plane, v, tile, pl.ds(row, 32), :] = (
                        got(start + 64 * v + 32 * tile) * there
                    )
                measured[plane, v, 2, pl.ds(row, 32), :] = (
                    sides(
                        turn(got(corner), 32 + 32 * v), turn(got(corner + 32), 32 - 32 * v)
                    )
                    * there
                )

    loads[0].wait()
    loads[1].wait()
    slot_rows, rank_rows, rank_columns, place_columns = [], [], [], []
    sub, lane = iota((128, 128), 0), iota((128, 128), 1)
    for v in range(2):
        row = slot_of(owners[pl.ds(v, 1), :], here)
        across = jnp.broadcast_to(row, (128, 128))
        same = across == across.T
        slot_rows.append(row)
        rank_rows.append(
            jnp.sum(jnp.where(same & (sub < lane), 1.0, 0.0), axis=0, keepdims=True).astype(
                jnp.int32
            )
        )
        rank_columns.append(
            jnp.sum(jnp.where(same & (lane < sub), 1.0, 0.0), axis=1, keepdims=True)
        )
        place = places[pl.ds(v, 1), :]
        spot = ((place & 7) * 32 + (place >> 3) + 1).astype(F32)
        place_columns.append(jnp.broadcast_to(spot, (128, 128)).T)

    lane_view, lane_rank, lane_part = (lane >> 3) & 1, (lane >> 2) & 1, lane & 3
    ids = jnp.zeros((128, 128), F32)
    for v in range(2):
        taken = jnp.where(sub == slot_rows[v], 1.0, 0.0).astype(BF16)
        mine = (lane_view == v) & (lane_rank.astype(F32) == rank_columns[v])
        ids = ids + dot(taken, jnp.where(mine, place_columns[v], 0.0).astype(BF16))
    ids = jnp.where(ids > 0.0, ids + (lane_view * 256 + lane_part * 8 - 1).astype(F32), -1.0)
    ids_out[...] = ids.reshape(128, 1, 128)

    target = jnp.concatenate(
        [
            slot_rows[v] * 16 + v * 8 + rank_rows[v] * 4 + part
            for v in range(2)
            for part in range(4)
        ],
        axis=1,
    )
    loads[3].wait()
    for plane in range(2):
        for v in range(2):
            for part in range(4):
                staged[plane, pl.ds((v * 4 + part) * 128, 128), :] = blocks[
                    v, :, pl.ds(plane * 1024 + part * 256, 256)
                ]
    loads[2].wait()
    for plane in range(2):
        pack_estimate(plane)

    def pick_group(plane, group):
        rows = GROUP * 16
        wanted = iota((rows, 1024), 0) + group * rows
        pick = jnp.where(wanted == target, 1.0, 0.0).astype(BF16)
        outgoing[plane, pl.ds(pl.multiple_of(group * rows, rows), rows), :] = dot(
            pick, staged[plane]
        ).astype(BF16)

    @pl.loop(0, GROUPS)
    def _(group):
        pick_group(0, group)

    pl.semaphore_wait(barrier, N_GX + N_GY - 2)
    for step in range(1, N_GY):
        pl.semaphore_signal(
            ready, inc=1, device_id=(gx, (gy + step) % N_GY), device_id_type=MESH
        )

    def id_copy(slot):
        return pltpu.make_async_remote_copy(
            src_ref=ids_out.at[pl.ds(slot, 1)],
            dst_ref=ids_in.at[pl.ds(slot, 1)],
            send_sem=ids_sent,
            recv_sem=ids_here,
            device_id=partner(slot, here),
            device_id_type=MESH,
        )

    def data_copy(plane, slot):
        rows = pl.ds(pl.multiple_of(slot * 16, 16), 16)
        return pltpu.make_async_remote_copy(
            src_ref=outgoing.at[plane, rows],
            dst_ref=incoming.at[plane, rows],
            send_sem=data_sent.at[plane],
            recv_sem=data_here.at[plane, slot // GROUP],
            device_id=partner(slot, here),
            device_id_type=MESH,
        )

    def send_group(group):
        for j in range(GROUP):
            if j == 0:

                @pl.when(group > 0)
                def _():
                    data_copy(1, group * GROUP).start()

            else:
                data_copy(1, group * GROUP + j).start()

    def send_first(to_x, to_y):
        slot = slot_of(to_x * N_GY + to_y, here)
        id_copy(slot).start()
        data_copy(0, slot).start()

    @pl.loop(1, N_GY)
    def _(step):
        send_first(gx, (gy + step) % N_GY)

    @pl.loop(1, N_GX)
    def _(step):
        send_first((gx + step) % N_GX, gy)

    pl.semaphore_wait(ready, N_GY - 1)
    for plane in range(2):
        send_parts(
            ESTIMATE_PARTS,
            estimate_out.at[plane],
            estimate_halo.at[plane],
            estimate_sent.at[plane],
            estimate_here.at[plane],
        )

    @pl.loop(1, DEVICES)
    def _(slot):
        to_x, to_y = partner(slot, here)

        @pl.when((to_x != gx) & (to_y != gy))
        def _():
            id_copy(slot).start()
            data_copy(0, slot).start()

    @pl.loop(0, GROUPS)
    def _(group):
        pick_group(1, group)
        send_group(group)

    for load in loads[4:]:
        load.wait()

    def bands(v, plane, axis, reverse):
        kernel_index = psf_index[v, plane]
        wide = iota((8, 512), 1)
        taps = jnp.zeros((8, 512), F32)
        total = jnp.zeros((8, 512), F32)
        for t in range(TAPS):
            value = psf_taps[v, kernel_index, axis, t]
            at = 88 + (TAPS - 1 - t if reverse else t)
            taps = jnp.where(wide == at, value, taps)
            total = total + value
        rows = jnp.broadcast_to((taps / total)[0:1], (WIDE, 512))
        return pltpu.roll(rows, 0, 1, stride=1, stride_axis=0)

    def by_lanes(m):
        at = iota((m.shape[0], 128), 1)
        side = jnp.where(
            at < 32, turn(m[:, :128], 32), jnp.where(at < 64, turn(m[:, 384:], 32), 0.0)
        )
        return jnp.concatenate([m[:, 128:384], side], axis=1)

    def by_rows(m):
        return jnp.concatenate([m[32 : 32 + TILE], m[:32], m[32 + TILE :]], axis=0)

    def reordered(m):
        for tile in range(4):
            shuffle[tile] = m[:, tile * 128 : (tile + 1) * 128]
        main = [
            jnp.concatenate(
                [
                    shuffle[tile, pl.ds(32 + q * 8 + x8, 8, stride=32), :]
                    for tile in range(4)
                ],
                axis=1,
            )
            for x8 in range(8)
            for q in range(4)
        ]
        return jnp.concatenate(main + [m[:32], m[32 + TILE :]], axis=0)

    def put(ref, index, value):
        high, low = split(value)
        ref[(0,) + index] = high
        ref[(1,) + index] = low

    for plane in range(2):
        for v in range(2):
            m = by_lanes(by_rows(bands(v, plane, 1, True)))
            put(fwd_y, (plane, slice(None), pl.ds(v * LANES, LANES)), m)
            put(back_y, (plane, v), by_lanes(by_rows(bands(v, plane, 1, False))))
            m = by_lanes(reordered(bands(v, plane, 0, False)))
            put(fwd_x, (plane, v), m[:, :WIDE])
            square = jnp.concatenate([m, jnp.zeros((LANES - WIDE, LANES), F32)], axis=0)
            put(back_x, (plane, v), square.T[:WIDE, :WIDE])

    def forward(field, plane):
        field = field.astype(BF16)[:, :WIDE]
        along_y = (dot(field, fwd_y[0, plane]) + dot(field, fwd_y[1, plane])).astype(BF16)
        blurred = []
        for v in range(2):
            mine = along_y[:, v * LANES : (v + 1) * LANES]
            blurred.append(
                dot(fwd_x[0, plane, v], mine)
                + dot(fwd_x[1, plane, v], mine)
                + background[v, plane]
            )
        return blurred

    def correction(ratios, plane, rows, lanes):
        total = jnp.zeros((rows, lanes), F32)
        for v in range(2):
            ratio = ratios[v].astype(BF16)[:, :WIDE]
            high, low = split(
                dot(ratio, back_y[0, plane, v][:, :lanes])
                + dot(ratio, back_y[1, plane, v][:, :lanes])
            )
            total = (
                total
                + dot(back_x[0, plane, v][:rows], high)
                + dot(back_x[0, plane, v][:rows], low)
                + dot(back_x[1, plane, v][:rows], high)
            )
        return total

    for plane in range(2):
        widen_estimate(plane)
        for v, blurred in enumerate(forward(wide_estimate[plane], plane)):
            inverse[plane, v] = 1.0 / blurred

    rest = ids_in.at[pl.ds(1, DEVICES - 1)]
    pltpu.make_async_copy(rest, rest, ids_here).wait()
    ids_in[pl.ds(0, 1)] = ids_out[pl.ds(0, 1)]
    spot = iota((512, 256), 0).astype(F32)
    picked = (iota((8, 128), 1) // 16) == iota((8, 128), 0)
    for group in range(GROUPS):
        halves = []
        for half in range(2):
            eight = ids_in[pl.ds(group * GROUP + half * 8, 8)].reshape(8, 128)
            halves.append(jnp.sum(jnp.where(picked, eight, 0.0), axis=0, keepdims=True))
        wanted = jnp.concatenate(halves, axis=1)
        landing[:, pl.ds(group * 256, 256)] = jnp.where(spot == wanted, 1.0, 0.0).astype(BF16)

    def land(plane):
        incoming[plane, pl.ds(0, 16)] = outgoing[plane, pl.ds(0, 16)]
        for group in range(GROUPS):
            first = group * 256
            came = (
                incoming.at[plane, pl.ds(16, 240)]
                if group == 0
                else incoming.at[plane, pl.ds(first, 256)]
            )
            pltpu.make_async_copy(came, came, data_here.at[plane, group]).wait()
            part = dot(
                landing[:, pl.ds(first, 256)], incoming[plane, pl.ds(first, 256), :]
            )
            summed[...] = part if group == 0 else summed[...] + part
        send_sides(plane)
        group_of = narrow // 32
        for v in range(2):
            for h in range(2):
                for wide in range(2):
                    source = [
                        summed[
                            pl.ds(v * 256 + (wide * 4 + by) * 32, 32), pl.ds(h * 128, 128)
                        ]
                        for by in range(4)
                    ]
                    for x4 in range(4):
                        tile = source[x4]
                        for by in range(4):
                            if by != x4:
                                moved = pltpu.roll(source[by], ((by - x4) % 4) * 32, 1)
                                tile = jnp.where(group_of == by, moved, tile)
                        measured[plane, v, wide, pl.ds((h * 4 + x4) * 32, 32), :] = tile

    def wide_measured(plane, v):
        return jnp.concatenate([measured[plane, v, tile] for tile in range(3)], axis=1)

    for plane in range(2):
        land(plane)
        send_others(plane)

    for plane in range(2):
        widen_measured(plane)
        ratios = [wide_measured(plane, v) * inverse[plane, v] for v in range(2)]
        current = wide_estimate[plane] * (0.5 * correction(ratios, plane, WIDE, LANES))
        ratios = [
            wide_measured(plane, v) / blurred for v, blurred in enumerate(forward(current, plane))
        ]
        result[plane] = current[:TILE, :TILE] * (
            0.5 * correction(ratios, plane, TILE, TILE)
        )

    rest = ids_out.at[pl.ds(1, DEVICES - 1)]
    pltpu.make_async_copy(rest, rest, ids_sent).wait()
    for plane in range(2):
        rest = outgoing.at[plane, pl.ds(16, (DEVICES - 1) * 16)]
        pltpu.make_async_copy(rest, rest, data_sent.at[plane]).wait()
        whole = estimate_out.at[plane]
        pltpu.make_async_copy(whole, whole, estimate_sent.at[plane]).wait()
        whole = measured_out.at[plane]
        pltpu.make_async_copy(whole, whole, measured_sent.at[plane]).wait()


def shards(blocks, owner_route, block_slot, estimate, background, psf_taps, psf_index):
    owners = owner_route.reshape(owner_route.shape[:2])
    far = pl.BlockSpec(memory_space=pltpu.HBM)
    dma = pltpu.SemaphoreType.DMA
    return pl.pallas_call(
        kernel,
        out_shape=jax.ShapeDtypeStruct(estimate.shape, F32),
        in_specs=[far] * 7,
        out_specs=pl.BlockSpec(memory_space=pltpu.VMEM),
        scratch_shapes=[
            pltpu.VMEM(blocks.shape, BF16),
            pltpu.VMEM(owners.shape, jnp.int32),
            pltpu.VMEM(block_slot.shape, jnp.int32),
            pltpu.VMEM(estimate.shape, F32),
            pltpu.SMEM(background.shape, F32),
            pltpu.SMEM(psf_taps.shape, F32),
            pltpu.SMEM(psf_index.shape, jnp.int32),
            pltpu.VMEM((2, 1024, 256), BF16),
            pltpu.VMEM((2, DEVICES * 16, 256), BF16),
            pltpu.VMEM((2, DEVICES * 16, 256), BF16),
            pltpu.VMEM((DEVICES, 1, 128), F32),
            pltpu.VMEM((DEVICES, 1, 128), F32),
            pltpu.VMEM((512, DEVICES * 16), BF16),
            pltpu.VMEM((512, 256), F32),
            pltpu.VMEM((2, WIDE, LANES), F32),
            pltpu.VMEM((2, 2, 3, WIDE, 128), F32),
            pltpu.VMEM((2, 2, WIDE, LANES), F32),
            pltpu.VMEM((4, WIDE, 128), F32),
            pltpu.VMEM((2, ESTIMATE_ROWS, 128), BF16),
            pltpu.VMEM((2, ESTIMATE_ROWS, 128), BF16),
            pltpu.VMEM((2, MEASURED_ROWS, 128), BF16),
            pltpu.VMEM((2, MEASURED_ROWS, 128), BF16),
            pltpu.VMEM((2, 2, WIDE, 2 * LANES), BF16),
            pltpu.VMEM((2, 2, 2, WIDE, WIDE), BF16),
            pltpu.VMEM((2, 2, 2, WIDE, LANES), BF16),
            pltpu.VMEM((2, 2, 2, WIDE, WIDE), BF16),
            pltpu.SemaphoreType.REGULAR,
            dma((7,)),
            dma((2,)),
            dma((2, GROUPS)),
            dma,
            dma,
            dma((2,)),
            dma((2,)),
            dma((2,)),
            dma((2,)),
        ],
        compiler_params=pltpu.CompilerParams(
            collective_id=0, has_side_effects=True, vmem_limit_bytes=62 << 20
        ),
        cost_estimate=pl.CostEstimate(
            flops=8_000_000_000, bytes_accessed=2 << 20, transcendentals=0
        ),
    )(blocks, owners, block_slot, estimate, background, psf_taps, psf_index)


def solution(mesh):
    return jax.shard_map(
        shards,
        mesh=mesh,
        in_specs=(
            P(None, ("gx", "gy"), None),
            P(None, ("gx", "gy"), None),
            P(None, ("gx", "gy")),
            P(None, "gx", "gy"),
            P(),
            P(),
            P(),
        ),
        out_specs=P(None, "gx", "gy"),
        check_vma=False,
    )
```

```python
import jax
import jax.numpy as jnp
from jax import lax
from jax.experimental import pallas as pl
from jax.experimental.pallas import tpu as pltpu
from jax.sharding import PartitionSpec as P

MESH = pl.DeviceIdType.MESH
F32 = jnp.float32
BF16 = jnp.bfloat16

N_GX, N_GY = 16, 8
DEVICES = N_GX * N_GY
TILE = 256
TAPS = 17
WIDE = TILE + 64
LANES = 384
STEP, STEP_INVERSE = 27, 19
GROUP = 16
GROUPS = DEVICES // GROUP
ESTIMATE_PARTS = (
    (0, 64, 1, 0),
    (64, 64, -1, 0),
    (128, 64, 0, 1),
    (192, 64, 0, -1),
    (256, 16, 1, 1),
    (272, 16, 1, -1),
    (288, 16, -1, 1),
    (304, 16, -1, -1),
)
ESTIMATE_ROWS = 320
SIDE_PARTS = ((256, 128, 0, 1), (384, 128, 0, -1))
OTHER_PARTS = (
    (0, 128, 1, 0),
    (128, 128, -1, 0),
    (512, 32, 1, 1),
    (544, 32, 1, -1),
    (576, 32, -1, 1),
    (608, 32, -1, -1),
)
MEASURED_ROWS = 640


def iota(shape, dim):
    return lax.broadcasted_iota(jnp.int32, shape, dim)


def dot(a, b):
    return jnp.dot(a, b, preferred_element_type=F32)


def split(a):
    high = a.astype(BF16)
    return high, (a - high.astype(F32)).astype(BF16)


def torus_position():
    gx, gy = lax.axis_index("gx"), lax.axis_index("gy")
    return gy // 2, ((gx // 2) % 2) * 2 + gy % 2, gx // 4, gx % 2


def partner(slot, here):
    x, y, z, core = here
    shift = (slot * STEP) % DEVICES
    core = (core + shift % 2) % 2
    x = (x + (shift // 2) % 4) % 4
    y = (y + (shift // 8) % 4) % 4
    z = (z + shift // 32) % 4
    return z * 4 + (y // 2) * 2 + core, x * 2 + y % 2


def slot_of(tile, here):
    x, y, z, core = here
    gx, gy = tile >> 3, tile & 7
    d_core = ((gx & 1) - core) & 1
    dx = ((gy >> 1) - x) & 3
    dy = ((((gx >> 1) & 1) * 2 + (gy & 1)) - y) & 3
    dz = ((gx >> 2) - z) & 3
    return ((d_core + 2 * dx + 8 * dy + 32 * dz) * STEP_INVERSE) & (DEVICES - 1)


def kernel(
    blocks_in,
    owners_in,
    places_in,
    estimate_in,
    background_in,
    taps_in,
    index_in,
    result,
    blocks,
    owners,
    places,
    estimate,
    background,
    psf_taps,
    psf_index,
    staged,
    outgoing,
    incoming,
    ids_out,
    ids_in,
    landing,
    summed,
    wide_estimate,
    measured,
    inverse,
    shuffle,
    estimate_out,
    estimate_halo,
    measured_out,
    measured_halo,
    fwd_y,
    fwd_x,
    back_y,
    back_x,
    ready,
    loaded,
    data_sent,
    data_here,
    ids_sent,
    ids_here,
    estimate_sent,
    estimate_here,
    measured_sent,
    measured_here,
):
    gx, gy = lax.axis_index("gx"), lax.axis_index("gy")
    here = torus_position()
    barrier = pltpu.get_barrier_semaphore()

    loads = [
        pltpu.make_async_copy(source, target, loaded.at[i])
        for i, (source, target) in enumerate(
            (
                (owners_in, owners),
                (places_in, places),
                (estimate_in, estimate),
                (blocks_in, blocks),
                (background_in, background),
                (taps_in, psf_taps),
                (index_in, psf_index),
            )
        )
    ]
    for load in loads:
        load.start()

    for step in (6, 10, 7, 9, 8, 2, 14, 3, 13, 5, 11, 4, 12, 15, 1):
        pl.semaphore_signal(
            barrier, inc=1, device_id=((gx + step) % N_GX, gy), device_id_type=MESH
        )
    for step in (5, 3, 4, 6, 2, 7, 1):
        pl.semaphore_signal(
            barrier, inc=1, device_id=(gx, (gy + step) % N_GY), device_id_type=MESH
        )

    has_low_x = jnp.where(gx > 0, 1.0, 0.0)
    has_high_x = jnp.where(gx < N_GX - 1, 1.0, 0.0)
    has_low_y = jnp.where(gy > 0, 1.0, 0.0)
    has_high_y = jnp.where(gy < N_GY - 1, 1.0, 0.0)
    narrow = iota((32, 128), 1)

    def turn(a, shift):
        return pltpu.roll(a, shift % 128, 1) if shift % 128 else a

    def sides(low, high):
        at = iota(low.shape, 1)
        both = jnp.where(
            at < 32, low * has_low_y, jnp.where(at < 64, high * has_high_y, 0.0)
        )
        return both + turn(both, 64)

    def send_parts(parts, out, into, sent, arrived):
        for start, rows, to_x, to_y in parts:
            pltpu.make_async_remote_copy(
                src_ref=out.at[pl.ds(start, rows)],
                dst_ref=into.at[pl.ds(start, rows)],
                send_sem=sent,
                recv_sem=arrived,
                device_id=((gx + to_x + N_GX) % N_GX, (gy + to_y + N_GY) % N_GY),
                device_id_type=MESH,
            ).start()

    def pack_estimate(plane):
        out = estimate_out.at[plane]
        for at, row in ((0, 224), (64, 0)):
            for tile in range(2):
                out[pl.ds(at + 32 * tile, 32)] = estimate[
                    plane, pl.ds(row, 32), pl.ds(128 * tile, 128)
                ].astype(BF16)
        for at, tile in ((128, 1), (192, 0)):
            packed = jnp.zeros((64, 128), F32)
            for slab in range(4):
                piece = estimate[plane, pl.ds(64 * slab, 64), pl.ds(128 * tile, 128)]
                moved = turn(piece, 32 * slab + 32 * tile)
                packed = jnp.where(iota((64, 128), 1) // 32 == slab, moved, packed)
            out[pl.ds(at, 64)] = packed.astype(BF16)
        for at, row, tile in ((256, 224, 1), (272, 224, 0), (288, 0, 1), (304, 0, 0)):
            top, bottom = (
                estimate[plane, pl.ds(row + 16 * half, 16), pl.ds(128 * tile, 128)]
                for half in range(2)
            )
            at_lane = iota((16, 128), 1)
            top, bottom = turn(top, 32 * tile), turn(bottom, 32 + 32 * tile)
            out[pl.ds(at, 16)] = jnp.where(at_lane < 32, top, bottom).astype(BF16)

    def widen_estimate(plane):
        whole = estimate_halo.at[plane]
        pltpu.make_async_copy(whole, whole, estimate_here.at[plane]).wait()

        def got(start, rows):
            return estimate_halo[plane, pl.ds(start, rows)].astype(F32)

        wide = wide_estimate.at[plane]
        wide[pl.ds(0, TILE), pl.ds(0, TILE)] = estimate[plane]
        for slab in range(4):
            wide[pl.ds(64 * slab, 64), pl.ds(TILE, 128)] = sides(
                turn(got(128, 64), -32 * slab), turn(got(192, 64), 32 - 32 * slab)
            )
        for row, start, corner, there in (
            (TILE, 0, 256, has_low_x),
            (TILE + 32, 64, 288, has_high_x),
        ):
            for tile in range(2):
                wide[pl.ds(row, 32), pl.ds(128 * tile, 128)] = (
                    got(start + 32 * tile, 32) * there
                )
            low, high = got(corner, 16), got(corner + 16, 16)
            wide[pl.ds(row, 16), pl.ds(TILE, 128)] = sides(low, turn(high, 32)) * there
            wide[pl.ds(row + 16, 16), pl.ds(TILE, 128)] = sides(turn(low, -32), high) * there

    def send_sides(plane):
        for at, by in ((256, 7), (384, 0)):
            for v in range(2):
                for h in range(2):
                    measured_out[plane, pl.ds(at + 64 * v + 32 * h, 32)] = summed[
                        pl.ds(v * 256 + by * 32, 32), pl.ds(128 * h, 128)
                    ].astype(BF16)
        send_parts(
            SIDE_PARTS,
            measured_out.at[plane],
            measured_halo.at[plane],
            measured_sent.at[plane],
            measured_here.at[plane],
        )

    def send_others(plane):
        out = measured_out.at[plane]

        def edge(v, tile, bx):
            return jnp.concatenate(
                [measured[plane, v, tile, pl.ds(q * 8 + bx, 8, stride=32), :] for q in range(4)], axis=0
            )

        for at, bx, corner in ((0, 7, 512), (128, 0, 576)):
            for tile in range(2):
                edges = [edge(v, tile, bx) for v in range(2)]
                for v in range(2):
                    out[pl.ds(at + 64 * v + 32 * tile, 32)] = edges[v].astype(BF16)
                if tile == 1:
                    both = jnp.where(narrow >= 96, edges[0], turn(edges[1], 96))
                    out[pl.ds(corner, 32)] = both.astype(BF16)
                else:
                    both = jnp.where(narrow < 32, edges[0], turn(edges[1], 32))
                    out[pl.ds(corner + 32, 32)] = both.astype(BF16)
        send_parts(
            OTHER_PARTS,
            measured_out.at[plane],
            measured_halo.at[plane],
            measured_sent.at[plane],
            measured_here.at[plane],
        )

    def widen_measured(plane):
        whole = measured_halo.at[plane]
        pltpu.make_async_copy(whole, whole, measured_here.at[plane]).wait()

        def got(start):
            return measured_halo[plane, pl.ds(start, 32)].astype(F32)

        for v in range(2):
            for x8 in range(8):
                at, back = 64 * v + 32 * (x8 // 4), -32 * (x8 % 4)
                measured[plane, v, 2, pl.ds(32 * x8, 32), :] = sides(
                    turn(got(256 + at), back), turn(got(384 + at), back + 32)
                )
            for row, start, corner, there in (
                (TILE, 0, 512, has_low_x),
                (TILE + 32, 128, 576, has_high_x),
            ):
                for tile in range(2):
                    measured[plane, v, tile, pl.ds(row, 32), :] = (
                        got(start + 64 * v + 32 * tile) * there
                    )
                measured[plane, v, 2, pl.ds(row, 32), :] = (
                    sides(
                        turn(got(corner), 32 + 32 * v), turn(got(corner + 32), 32 - 32 * v)
                    )
                    * there
                )

    loads[0].wait()
    loads[1].wait()
    slot_rows, rank_rows, rank_columns, place_columns = [], [], [], []
    sub, lane = iota((128, 128), 0), iota((128, 128), 1)
    for v in range(2):
        row = slot_of(owners[pl.ds(v, 1), :], here)
        across = jnp.broadcast_to(row, (128, 128))
        same = across == across.T
        slot_rows.append(row)
        rank_rows.append(
            jnp.sum(jnp.where(same & (sub < lane), 1.0, 0.0), axis=0, keepdims=True).astype(
                jnp.int32
            )
        )
        rank_columns.append(
            jnp.sum(jnp.where(same & (lane < sub), 1.0, 0.0), axis=1, keepdims=True)
        )
        place = places[pl.ds(v, 1), :]
        spot = ((place & 7) * 32 + (place >> 3) + 1).astype(F32)
        place_columns.append(jnp.broadcast_to(spot, (128, 128)).T)

    lane_view, lane_rank, lane_part = (lane >> 3) & 1, (lane >> 2) & 1, lane & 3
    ids = jnp.zeros((128, 128), F32)
    for v in range(2):
        taken = jnp.where(sub == slot_rows[v], 1.0, 0.0).astype(BF16)
        mine = (lane_view == v) & (lane_rank.astype(F32) == rank_columns[v])
        ids = ids + dot(taken, jnp.where(mine, place_columns[v], 0.0).astype(BF16))
    ids = jnp.where(ids > 0.0, ids + (lane_view * 256 + lane_part * 8 - 1).astype(F32), -1.0)
    ids_out[...] = ids.reshape(128, 1, 128)

    target = jnp.concatenate(
        [
            slot_rows[v] * 16 + v * 8 + rank_rows[v] * 4 + part
            for v in range(2)
            for part in range(4)
        ],
        axis=1,
    )
    loads[3].wait()
    for plane in range(2):
        for v in range(2):
            for part in range(4):
                staged[plane, pl.ds((v * 4 + part) * 128, 128), :] = blocks[
                    v, :, pl.ds(plane * 1024 + part * 256, 256)
                ]
    loads[2].wait()
    for plane in range(2):
        pack_estimate(plane)

    def pick_group(plane, group):
        rows = GROUP * 16
        wanted = iota((rows, 1024), 0) + group * rows
        pick = jnp.where(wanted == target, 1.0, 0.0).astype(BF16)
        outgoing[plane, pl.ds(pl.multiple_of(group * rows, rows), rows), :] = dot(
            pick, staged[plane]
        ).astype(BF16)

    @pl.loop(0, GROUPS)
    def _(group):
        pick_group(0, group)

    pl.semaphore_wait(barrier, N_GX + N_GY - 2)
    for step in range(1, N_GY):
        pl.semaphore_signal(
            ready, inc=1, device_id=(gx, (gy + step) % N_GY), device_id_type=MESH
        )

    def id_copy(slot):
        return pltpu.make_async_remote_copy(
            src_ref=ids_out.at[pl.ds(slot, 1)],
            dst_ref=ids_in.at[pl.ds(slot, 1)],
            send_sem=ids_sent,
            recv_sem=ids_here,
            device_id=partner(slot, here),
            device_id_type=MESH,
        )

    def data_copy(plane, slot):
        rows = pl.ds(pl.multiple_of(slot * 16, 16), 16)
        return pltpu.make_async_remote_copy(
            src_ref=outgoing.at[plane, rows],
            dst_ref=incoming.at[plane, rows],
            send_sem=data_sent.at[plane],
            recv_sem=data_here.at[plane, slot // GROUP],
            device_id=partner(slot, here),
            device_id_type=MESH,
        )

    def send_group(group):
        for j in range(GROUP):
            if j == 0:

                @pl.when(group > 0)
                def _():
                    data_copy(1, group * GROUP).start()

            else:
                data_copy(1, group * GROUP + j).start()

    def send_first(to_x, to_y):
        slot = slot_of(to_x * N_GY + to_y, here)
        id_copy(slot).start()
        data_copy(0, slot).start()

    @pl.loop(1, N_GY)
    def _(step):
        send_first(gx, (gy + step) % N_GY)

    @pl.loop(1, N_GX)
    def _(step):
        send_first((gx + step) % N_GX, gy)

    def send_estimate(parts):
        for plane in range(2):
            send_parts(
                parts,
                estimate_out.at[plane],
                estimate_halo.at[plane],
                estimate_sent.at[plane],
                estimate_here.at[plane],
            )

    send_estimate(ESTIMATE_PARTS[:4])
    pl.semaphore_wait(ready, N_GY - 1)
    send_estimate(ESTIMATE_PARTS[4:])

    @pl.loop(1, DEVICES)
    def _(slot):
        to_x, to_y = partner(slot, here)

        @pl.when((to_x != gx) & (to_y != gy))
        def _():
            id_copy(slot).start()
            data_copy(0, slot).start()

    @pl.loop(0, GROUPS)
    def _(group):
        pick_group(1, group)
        send_group(group)

    for load in loads[4:]:
        load.wait()

    def bands(v, plane, axis, reverse):
        kernel_index = psf_index[v, plane]
        wide = iota((8, 512), 1)
        taps = jnp.zeros((8, 512), F32)
        total = jnp.zeros((8, 512), F32)
        for t in range(TAPS):
            value = psf_taps[v, kernel_index, axis, t]
            at = 88 + (TAPS - 1 - t if reverse else t)
            taps = jnp.where(wide == at, value, taps)
            total = total + value
        rows = jnp.broadcast_to((taps / total)[0:1], (WIDE, 512))
        return pltpu.roll(rows, 0, 1, stride=1, stride_axis=0)

    def by_lanes(m):
        at = iota((m.shape[0], 128), 1)
        side = jnp.where(
            at < 32, turn(m[:, :128], 32), jnp.where(at < 64, turn(m[:, 384:], 32), 0.0)
        )
        return jnp.concatenate([m[:, 128:384], side + turn(side, 64)], axis=1)

    def by_rows(m):
        return jnp.concatenate([m[32 : 32 + TILE], m[:32], m[32 + TILE :]], axis=0)

    def reordered(m):
        for tile in range(4):
            shuffle[tile] = m[:, tile * 128 : (tile + 1) * 128]
        main = [
            jnp.concatenate(
                [
                    shuffle[tile, pl.ds(32 + q * 8 + x8, 8, stride=32), :]
                    for tile in range(4)
                ],
                axis=1,
            )
            for x8 in range(8)
            for q in range(4)
        ]
        return jnp.concatenate(main + [m[:32], m[32 + TILE :]], axis=0)

    def rounded_sum(first):
        return jnp.sum(first[0:1].astype(BF16).astype(F32), axis=1, keepdims=True)

    scales = []
    for plane in range(2):
        for v in range(2):
            m = by_lanes(by_rows(bands(v, plane, 1, True)))
            fwd_y[plane, :, pl.ds(v * LANES, LANES)] = m.astype(BF16)
            m = bands(v, plane, 1, False)
            scale = rounded_sum(m)
            high, low = split(by_lanes(by_rows(m)))
            back_y[plane, v] = jnp.concatenate([high, low[TILE:], low[:TILE]], axis=0)
            m = bands(v, plane, 0, False)
            scales.append(1.0 / (scale * rounded_sum(m)))
            m = by_lanes(reordered(m))
            fwd_x[plane, v] = m[:, :WIDE].astype(BF16)
            square = jnp.concatenate([m, jnp.zeros((LANES - WIDE, LANES), F32)], axis=0)
            high, low = split(square.T[:WIDE])
            side = high[:, TILE:].astype(F32)
            side = (side + turn(side, 64)).astype(BF16)
            for at, piece in (
                (0, high[:, :TILE]),
                (TILE, high[:, :TILE]),
                (2 * TILE, low[:, :TILE]),
                (3 * TILE, side),
                (3 * TILE + 128, low[:, TILE:]),
            ):
                back_x[plane, v, :, pl.ds(at, piece.shape[1])] = piece

    def forward(field, plane):
        field = field.astype(BF16)[:, :WIDE]
        along_y = dot(field, fwd_y[plane]).astype(BF16)
        return [
            dot(fwd_x[plane, v], along_y[:, v * LANES : (v + 1) * LANES])
            * scales[2 * plane + v]
            + background[v, plane]
            for v in range(2)
        ]

    def correction(ratios, plane, rows, lanes):
        total = jnp.zeros((rows, lanes), F32)
        for v in range(2):
            ratio = ratios[v].astype(BF16)
            ratio = jnp.concatenate([ratio, ratio[:, :TILE]], axis=1)
            high, low = split(dot(ratio, back_y[plane, v][:, :lanes]))
            stack = [high[:TILE], low[:TILE], high[:TILE], high[TILE:], low[TILE:], high[TILE:]]
            total = total + dot(
                back_x[plane, v][:rows, : 3 * WIDE], jnp.concatenate(stack, axis=0)
            )
        return total

    for plane in range(2):
        widen_estimate(plane)
        for v, blurred in enumerate(forward(wide_estimate[plane], plane)):
            inverse[plane, v] = 1.0 / blurred

    rest = ids_in.at[pl.ds(1, DEVICES - 1)]
    pltpu.make_async_copy(rest, rest, ids_here).wait()
    ids_in[pl.ds(0, 1)] = ids_out[pl.ds(0, 1)]
    spot = iota((512, 256), 0).astype(F32)
    picked = (iota((8, 128), 1) // 16) == iota((8, 128), 0)
    for group in range(GROUPS):
        halves = []
        for half in range(2):
            eight = ids_in[pl.ds(group * GROUP + half * 8, 8)].reshape(8, 128)
            halves.append(jnp.sum(jnp.where(picked, eight, 0.0), axis=0, keepdims=True))
        wanted = jnp.concatenate(halves, axis=1)
        landing[:, pl.ds(group * 256, 256)] = jnp.where(spot == wanted, 1.0, 0.0).astype(BF16)

    def land(plane):
        incoming[plane, pl.ds(0, 16)] = outgoing[plane, pl.ds(0, 16)]
        for group in range(GROUPS):
            first = group * 256
            came = (
                incoming.at[plane, pl.ds(16, 240)]
                if group == 0
                else incoming.at[plane, pl.ds(first, 256)]
            )
            pltpu.make_async_copy(came, came, data_here.at[plane, group]).wait()
            part = dot(
                landing[:, pl.ds(first, 256)], incoming[plane, pl.ds(first, 256), :]
            )
            summed[...] = part if group == 0 else summed[...] + part
        send_sides(plane)
        group_of = narrow // 32
        for v in range(2):
            for h in range(2):
                for wide in range(2):
                    source = [
                        summed[
                            pl.ds(v * 256 + (wide * 4 + by) * 32, 32), pl.ds(h * 128, 128)
                        ]
                        for by in range(4)
                    ]
                    for x4 in range(4):
                        tile = source[x4]
                        for by in range(4):
                            if by != x4:
                                moved = pltpu.roll(source[by], ((by - x4) % 4) * 32, 1)
                                tile = jnp.where(group_of == by, moved, tile)
                        measured[plane, v, wide, pl.ds((h * 4 + x4) * 32, 32), :] = tile

    def wide_measured(plane, v):
        return jnp.concatenate([measured[plane, v, tile] for tile in range(3)], axis=1)

    for plane in range(2):
        land(plane)
        send_others(plane)

    for plane in range(2):
        widen_measured(plane)
        ratios = [wide_measured(plane, v) * inverse[plane, v] for v in range(2)]
        current = wide_estimate[plane] * (0.5 * correction(ratios, plane, WIDE, LANES))
        ratios = [
            wide_measured(plane, v) / blurred for v, blurred in enumerate(forward(current, plane))
        ]
        result[plane] = current[:TILE, :TILE] * (
            0.5 * correction(ratios, plane, TILE, TILE)
        )

    rest = ids_out.at[pl.ds(1, DEVICES - 1)]
    pltpu.make_async_copy(rest, rest, ids_sent).wait()
    for plane in range(2):
        rest = outgoing.at[plane, pl.ds(16, (DEVICES - 1) * 16)]
        pltpu.make_async_copy(rest, rest, data_sent.at[plane]).wait()
        whole = estimate_out.at[plane]
        pltpu.make_async_copy(whole, whole, estimate_sent.at[plane]).wait()
        whole = measured_out.at[plane]
        pltpu.make_async_copy(whole, whole, measured_sent.at[plane]).wait()


def shards(blocks, owner_route, block_slot, estimate, background, psf_taps, psf_index):
    owners = owner_route.reshape(owner_route.shape[:2])
    far = pl.BlockSpec(memory_space=pltpu.HBM)
    dma = pltpu.SemaphoreType.DMA
    return pl.pallas_call(
        kernel,
        out_shape=jax.ShapeDtypeStruct(estimate.shape, F32),
        in_specs=[far] * 7,
        out_specs=pl.BlockSpec(memory_space=pltpu.VMEM),
        scratch_shapes=[
            pltpu.VMEM(blocks.shape, BF16),
            pltpu.VMEM(owners.shape, jnp.int32),
            pltpu.VMEM(block_slot.shape, jnp.int32),
            pltpu.VMEM(estimate.shape, F32),
            pltpu.SMEM(background.shape, F32),
            pltpu.SMEM(psf_taps.shape, F32),
            pltpu.SMEM(psf_index.shape, jnp.int32),
            pltpu.VMEM((2, 1024, 256), BF16),
            pltpu.VMEM((2, DEVICES * 16, 256), BF16),
            pltpu.VMEM((2, DEVICES * 16, 256), BF16),
            pltpu.VMEM((DEVICES, 1, 128), F32),
            pltpu.VMEM((DEVICES, 1, 128), F32),
            pltpu.VMEM((512, DEVICES * 16), BF16),
            pltpu.VMEM((512, 256), F32),
            pltpu.VMEM((2, WIDE, LANES), F32),
            pltpu.VMEM((2, 2, 3, WIDE, 128), F32),
            pltpu.VMEM((2, 2, WIDE, LANES), F32),
            pltpu.VMEM((4, WIDE, 128), F32),
            pltpu.VMEM((2, ESTIMATE_ROWS, 128), BF16),
            pltpu.VMEM((2, ESTIMATE_ROWS, 128), BF16),
            pltpu.VMEM((2, MEASURED_ROWS, 128), BF16),
            pltpu.VMEM((2, MEASURED_ROWS, 128), BF16),
            pltpu.VMEM((2, WIDE, 2 * LANES), BF16),
            pltpu.VMEM((2, 2, WIDE, WIDE), BF16),
            pltpu.VMEM((2, 2, 2 * WIDE, LANES), BF16),
            pltpu.VMEM((2, 2, WIDE, 1024), BF16),
            pltpu.SemaphoreType.REGULAR,
            dma((7,)),
            dma((2,)),
            dma((2, GROUPS)),
            dma,
            dma,
            dma((2,)),
            dma((2,)),
            dma((2,)),
            dma((2,)),
        ],
        compiler_params=pltpu.CompilerParams(
            collective_id=0, has_side_effects=True, vmem_limit_bytes=62 << 20
        ),
        cost_estimate=pl.CostEstimate(
            flops=8_000_000_000, bytes_accessed=2 << 20, transcendentals=0
        ),
    )(blocks, owners, block_slot, estimate, background, psf_taps, psf_index)


def solution(mesh):
    return jax.shard_map(
        shards,
        mesh=mesh,
        in_specs=(
            P(None, ("gx", "gy"), None),
            P(None, ("gx", "gy"), None),
            P(None, ("gx", "gy")),
            P(None, "gx", "gy"),
            P(),
            P(),
            P(),
        ),
        out_specs=P(None, "gx", "gy"),
        check_vma=False,
    )
```

```python
import jax
import jax.numpy as jnp
from jax import lax
from jax.experimental import pallas as pl
from jax.experimental.pallas import tpu as pltpu
from jax.sharding import PartitionSpec as P

MESH = pl.DeviceIdType.MESH
F32 = jnp.float32
BF16 = jnp.bfloat16

N_GX, N_GY = 16, 8
DEVICES = N_GX * N_GY
TILE = 256
TAPS = 17
WIDE = TILE + 64
LANES = 384
STEP, STEP_INVERSE = 27, 19
GROUP = 16
GROUPS = DEVICES // GROUP
ESTIMATE_PARTS = (
    (0, 64, 1, 0),
    (64, 64, -1, 0),
    (128, 64, 0, 1),
    (192, 64, 0, -1),
    (256, 16, 1, 1),
    (272, 16, 1, -1),
    (288, 16, -1, 1),
    (304, 16, -1, -1),
)
ESTIMATE_ROWS = 320
SIDE_PARTS = ((192, 128, 0, 1), (320, 128, 0, -1))
OTHER_PARTS = (
    (0, 96, 1, 0),
    (96, 96, -1, 0),
    (448, 16, 1, 1),
    (464, 16, 1, -1),
    (480, 16, -1, 1),
    (496, 16, -1, -1),
)
MEASURED_ROWS = 512


def iota(shape, dim):
    return lax.broadcasted_iota(jnp.int32, shape, dim)


def dot(a, b):
    return jnp.dot(a, b, preferred_element_type=F32)


def split(a):
    high = a.astype(BF16)
    return high, (a - high.astype(F32)).astype(BF16)


def torus_position():
    gx, gy = lax.axis_index("gx"), lax.axis_index("gy")
    return gy // 2, ((gx // 2) % 2) * 2 + gy % 2, gx // 4, gx % 2


def partner(slot, here):
    x, y, z, core = here
    shift = (slot * STEP) % DEVICES
    core = (core + shift % 2) % 2
    x = (x + (shift // 2) % 4) % 4
    y = (y + (shift // 8) % 4) % 4
    z = (z + shift // 32) % 4
    return z * 4 + (y // 2) * 2 + core, x * 2 + y % 2


def slot_of(tile, here):
    x, y, z, core = here
    gx, gy = tile >> 3, tile & 7
    d_core = ((gx & 1) - core) & 1
    dx = ((gy >> 1) - x) & 3
    dy = ((((gx >> 1) & 1) * 2 + (gy & 1)) - y) & 3
    dz = ((gx >> 2) - z) & 3
    return ((d_core + 2 * dx + 8 * dy + 32 * dz) * STEP_INVERSE) & (DEVICES - 1)


def kernel(
    blocks_in,
    owners_in,
    places_in,
    estimate_in,
    background_in,
    taps_in,
    index_in,
    result,
    blocks,
    owners,
    places,
    estimate,
    background,
    psf_taps,
    psf_index,
    staged,
    outgoing,
    incoming,
    ids_out,
    ids_in,
    landing,
    summed,
    wide_estimate,
    measured,
    inverse,
    final,
    shuffle,
    estimate_out,
    estimate_halo,
    measured_out,
    measured_halo,
    fwd_y,
    fwd_x,
    back_y,
    back_x,
    ready,
    loaded,
    stored,
    data_sent,
    data_here,
    ids_sent,
    ids_here,
    estimate_sent,
    estimate_here,
    measured_sent,
    measured_here,
):
    gx, gy = lax.axis_index("gx"), lax.axis_index("gy")
    here = torus_position()
    barrier = pltpu.get_barrier_semaphore()

    loads = [
        pltpu.make_async_copy(source, target, loaded.at[i])
        for i, (source, target) in enumerate(
            (
                (owners_in, owners),
                (places_in, places),
                (estimate_in, estimate),
                (blocks_in, blocks),
                (background_in, background),
                (taps_in, psf_taps),
                (index_in, psf_index),
            )
        )
    ]
    for step in (6, 10, 7, 9, 8, 2, 14, 3, 13, 5, 11, 4, 12, 15, 1):
        pl.semaphore_signal(
            barrier, inc=1, device_id=((gx + step) % N_GX, gy), device_id_type=MESH
        )
    for step in (5, 3, 4, 6, 2, 7, 1):
        pl.semaphore_signal(
            barrier, inc=1, device_id=(gx, (gy + step) % N_GY), device_id_type=MESH
        )

    for load in loads:
        load.start()

    has_low_x = jnp.where(gx > 0, 1.0, 0.0)
    has_high_x = jnp.where(gx < N_GX - 1, 1.0, 0.0)
    has_low_y = jnp.where(gy > 0, 1.0, 0.0)
    has_high_y = jnp.where(gy < N_GY - 1, 1.0, 0.0)
    narrow = iota((32, 128), 1)

    def turn(a, shift):
        return pltpu.roll(a, shift % 128, 1) if shift % 128 else a

    def sides(low, high):
        at = iota(low.shape, 1)
        both = jnp.where(
            at < 32, low * has_low_y, jnp.where(at < 64, high * has_high_y, 0.0)
        )
        return both + turn(both, 64)

    def send_parts(parts, out, into, sent, arrived):
        for start, rows, to_x, to_y in parts:
            pltpu.make_async_remote_copy(
                src_ref=out.at[pl.ds(start, rows)],
                dst_ref=into.at[pl.ds(start, rows)],
                send_sem=sent,
                recv_sem=arrived,
                device_id=((gx + to_x + N_GX) % N_GX, (gy + to_y + N_GY) % N_GY),
                device_id_type=MESH,
            ).start()

    def pack_estimate(plane):
        out = estimate_out.at[plane]
        for at, row in ((0, 224), (64, 0)):
            for tile in range(2):
                out[pl.ds(at + 32 * tile, 32)] = estimate[
                    plane, pl.ds(row, 32), pl.ds(128 * tile, 128)
                ].astype(BF16)
        for at, tile in ((128, 1), (192, 0)):
            packed = jnp.zeros((64, 128), F32)
            for slab in range(4):
                piece = estimate[plane, pl.ds(64 * slab, 64), pl.ds(128 * tile, 128)]
                moved = turn(piece, 32 * slab + 32 * tile)
                packed = jnp.where(iota((64, 128), 1) // 32 == slab, moved, packed)
            out[pl.ds(at, 64)] = packed.astype(BF16)
        for at, row, tile in ((256, 224, 1), (272, 224, 0), (288, 0, 1), (304, 0, 0)):
            top, bottom = (
                estimate[plane, pl.ds(row + 16 * half, 16), pl.ds(128 * tile, 128)]
                for half in range(2)
            )
            at_lane = iota((16, 128), 1)
            top, bottom = turn(top, 32 * tile), turn(bottom, 32 + 32 * tile)
            out[pl.ds(at, 16)] = jnp.where(at_lane < 32, top, bottom).astype(BF16)

    def widen_estimate(plane):
        whole = estimate_halo.at[plane]
        pltpu.make_async_copy(whole, whole, estimate_here.at[plane]).wait()

        def got(start, rows):
            return estimate_halo[plane, pl.ds(start, rows)].astype(F32)

        wide = wide_estimate.at[plane]
        wide[pl.ds(0, TILE), pl.ds(0, TILE)] = estimate[plane]
        for slab in range(4):
            wide[pl.ds(64 * slab, 64), pl.ds(TILE, 128)] = sides(
                turn(got(128, 64), -32 * slab), turn(got(192, 64), 32 - 32 * slab)
            )
        for row, start, corner, there in (
            (TILE, 0, 256, has_low_x),
            (TILE + 32, 64, 288, has_high_x),
        ):
            for tile in range(2):
                wide[pl.ds(row, 32), pl.ds(128 * tile, 128)] = (
                    got(start + 32 * tile, 32) * there
                )
            low, high = got(corner, 16), got(corner + 16, 16)
            wide[pl.ds(row, 16), pl.ds(TILE, 128)] = sides(low, turn(high, 32)) * there
            wide[pl.ds(row + 16, 16), pl.ds(TILE, 128)] = sides(turn(low, -32), high) * there

    def send_sides(plane):
        for at, by in ((192, 7), (320, 0)):
            for v in range(2):
                for h in range(2):
                    measured_out[plane, pl.ds(at + 64 * v + 32 * h, 32)] = summed[
                        pl.ds(v * 256 + by * 32, 32), pl.ds(128 * h, 128)
                    ].astype(BF16)
        send_parts(
            SIDE_PARTS,
            measured_out.at[plane],
            measured_halo.at[plane],
            measured_sent.at[plane],
            measured_here.at[plane],
        )

    def send_others(plane):
        out = measured_out.at[plane]

        def edge(v, tile, bx):
            return jnp.concatenate(
                [measured[plane, v, tile, pl.ds(q * 8 + bx, 8, stride=32), :] for q in range(4)], axis=0
            )

        for at, bx, corner, first in ((0, 7, 448, 8), (96, 0, 480, 0)):
            edges = [[edge(v, tile, bx) for tile in range(2)] for v in range(2)]
            out[pl.ds(at, 96)] = jnp.concatenate(
                [edges[v][tile][first : first + 24] for v in range(2) for tile in range(2)],
                axis=0,
            ).astype(BF16)
            for start, tile in ((corner, 1), (corner + 16, 0)):
                both = jnp.where(
                    narrow < 32,
                    turn(edges[0][tile], 32 * tile),
                    turn(edges[1][tile], 32 + 32 * tile),
                )
                out[pl.ds(start, 16)] = jnp.where(
                    narrow[:16] < 64, both[:16], turn(both[16:], 64)
                ).astype(BF16)
        send_parts(
            OTHER_PARTS,
            measured_out.at[plane],
            measured_halo.at[plane],
            measured_sent.at[plane],
            measured_here.at[plane],
        )

    def widen_measured(plane):
        whole = measured_halo.at[plane]
        pltpu.make_async_copy(whole, whole, measured_here.at[plane]).wait()

        def got(start, rows):
            return measured_halo[plane, pl.ds(start, rows)].astype(F32)

        for v in range(2):
            for x8 in range(8):
                at, back = 64 * v + 32 * (x8 // 4), -32 * (x8 % 4)
                measured[plane, v, 2, pl.ds(32 * x8, 32), :] = sides(
                    turn(got(192 + at, 32), back), turn(got(320 + at, 32), back + 32)
                )
        for row, first, start, corner, there in (
            (TILE, TILE + 8, 0, 448, has_low_x),
            (TILE + 32, TILE + 32, 96, 480, has_high_x),
        ):
            rows = got(start, 96) * there
            low, high = got(corner, 16), got(corner + 16, 16)
            for v in range(2):
                for tile in range(2):
                    at = 48 * v + 24 * tile
                    measured[plane, v, tile, pl.ds(first, 24), :] = rows[at : at + 24]
                for half in range(2):
                    back = -32 * v - 64 * half
                    measured[plane, v, 2, pl.ds(row + 16 * half, 16), :] = (
                        sides(turn(low, back), turn(high, back + 32)) * there
                    )

    loads[0].wait()
    loads[1].wait()
    slot_rows, rank_rows, rank_columns, place_columns = [], [], [], []
    sub, lane = iota((128, 128), 0), iota((128, 128), 1)
    for v in range(2):
        row = slot_of(owners[pl.ds(v, 1), :], here)
        across = jnp.broadcast_to(row, (128, 128))
        same = across == across.T
        slot_rows.append(row)
        rank_rows.append(
            jnp.sum(jnp.where(same & (sub < lane), 1.0, 0.0), axis=0, keepdims=True).astype(
                jnp.int32
            )
        )
        rank_columns.append(
            jnp.sum(jnp.where(same & (lane < sub), 1.0, 0.0), axis=1, keepdims=True)
        )
        place = places[pl.ds(v, 1), :]
        spot = ((place & 7) * 32 + (place >> 3) + 1).astype(F32)
        place_columns.append(jnp.broadcast_to(spot, (128, 128)).T)

    lane_view, lane_rank, lane_part = (lane >> 3) & 1, (lane >> 2) & 1, lane & 3
    ids = jnp.zeros((128, 128), F32)
    for v in range(2):
        taken = jnp.where(sub == slot_rows[v], 1.0, 0.0).astype(BF16)
        mine = (lane_view == v) & (lane_rank.astype(F32) == rank_columns[v])
        ids = ids + dot(taken, jnp.where(mine, place_columns[v], 0.0).astype(BF16))
    ids = jnp.where(ids > 0.0, ids + (lane_view * 256 + lane_part * 8 - 1).astype(F32), -1.0)
    ids_out[...] = ids.reshape(128, 1, 128)

    target = jnp.concatenate(
        [
            slot_rows[v] * 16 + v * 8 + rank_rows[v] * 4 + part
            for v in range(2)
            for part in range(4)
        ],
        axis=1,
    )
    loads[3].wait()
    for plane in range(2):
        for v in range(2):
            for part in range(4):
                staged[plane, pl.ds((v * 4 + part) * 128, 128), :] = blocks[
                    v, :, pl.ds(plane * 1024 + part * 256, 256)
                ]
    loads[2].wait()
    for plane in range(2):
        pack_estimate(plane)

    def pick_group(plane, group):
        rows = GROUP * 16
        wanted = iota((rows, 1024), 0) + group * rows
        pick = jnp.where(wanted == target, 1.0, 0.0).astype(BF16)
        outgoing[plane, pl.ds(pl.multiple_of(group * rows, rows), rows), :] = dot(
            pick, staged[plane]
        ).astype(BF16)

    @pl.loop(0, GROUPS)
    def _(group):
        pick_group(0, group)

    pl.semaphore_wait(barrier, N_GX + N_GY - 2)
    for step in range(1, N_GY):
        pl.semaphore_signal(
            ready, inc=1, device_id=(gx, (gy + step) % N_GY), device_id_type=MESH
        )

    def id_copy(slot):
        return pltpu.make_async_remote_copy(
            src_ref=ids_out.at[pl.ds(slot, 1)],
            dst_ref=ids_in.at[pl.ds(slot, 1)],
            send_sem=ids_sent,
            recv_sem=ids_here,
            device_id=partner(slot, here),
            device_id_type=MESH,
        )

    def data_copy(plane, slot):
        rows = pl.ds(pl.multiple_of(slot * 16, 16), 16)
        return pltpu.make_async_remote_copy(
            src_ref=outgoing.at[plane, rows],
            dst_ref=incoming.at[plane, rows],
            send_sem=data_sent.at[plane],
            recv_sem=data_here.at[plane, slot // GROUP],
            device_id=partner(slot, here),
            device_id_type=MESH,
        )

    def send_group(group):
        for j in range(GROUP):
            if j == 0:

                @pl.when(group > 0)
                def _():
                    data_copy(1, group * GROUP).start()

            else:
                data_copy(1, group * GROUP + j).start()

    def send_first(to_x, to_y):
        slot = slot_of(to_x * N_GY + to_y, here)
        id_copy(slot).start()
        data_copy(0, slot).start()

    @pl.loop(1, N_GY)
    def _(step):
        send_first(gx, (gy + step) % N_GY)

    @pl.loop(1, N_GX)
    def _(step):
        send_first((gx + step) % N_GX, gy)

    def send_estimate(parts):
        for plane in range(2):
            send_parts(
                parts,
                estimate_out.at[plane],
                estimate_halo.at[plane],
                estimate_sent.at[plane],
                estimate_here.at[plane],
            )

    send_estimate(ESTIMATE_PARTS[:4])
    pl.semaphore_wait(ready, N_GY - 1)
    send_estimate(ESTIMATE_PARTS[4:])

    @pl.loop(1, DEVICES)
    def _(slot):
        to_x, to_y = partner(slot, here)

        @pl.when((to_x != gx) & (to_y != gy))
        def _():
            id_copy(slot).start()
            data_copy(0, slot).start()

    @pl.loop(0, GROUPS)
    def _(group):
        pick_group(1, group)
        send_group(group)

    for load in loads[4:]:
        load.wait()

    def bands(v, plane, axis, reverse):
        kernel_index = psf_index[v, plane]
        wide = iota((8, 512), 1)
        taps = jnp.zeros((8, 512), F32)
        total = jnp.zeros((8, 512), F32)
        for t in range(TAPS):
            value = psf_taps[v, kernel_index, axis, t]
            at = 88 + (TAPS - 1 - t if reverse else t)
            taps = jnp.where(wide == at, value, taps)
            total = total + value
        rows = jnp.broadcast_to((taps / total)[0:1], (WIDE, 512))
        return pltpu.roll(rows, 0, 1, stride=1, stride_axis=0)

    def by_lanes(m):
        at = iota((m.shape[0], 128), 1)
        side = jnp.where(
            at < 32, turn(m[:, :128], 32), jnp.where(at < 64, turn(m[:, 384:], 32), 0.0)
        )
        return jnp.concatenate([m[:, 128:384], side + turn(side, 64)], axis=1)

    def by_rows(m):
        return jnp.concatenate([m[32 : 32 + TILE], m[:32], m[32 + TILE :]], axis=0)

    def reordered(m):
        for tile in range(4):
            shuffle[tile] = m[:, tile * 128 : (tile + 1) * 128]
        main = [
            jnp.concatenate(
                [
                    shuffle[tile, pl.ds(32 + q * 8 + x8, 8, stride=32), :]
                    for tile in range(4)
                ],
                axis=1,
            )
            for x8 in range(8)
            for q in range(4)
        ]
        return jnp.concatenate(main + [m[:32], m[32 + TILE :]], axis=0)

    def rounded_sum(first):
        return jnp.sum(first[0:1].astype(BF16).astype(F32), axis=1, keepdims=True)

    scales = []
    for plane in range(2):
        for v in range(2):
            m = by_lanes(by_rows(bands(v, plane, 1, True)))
            fwd_y[plane, :, pl.ds(v * LANES, LANES)] = m.astype(BF16)
            m = bands(v, plane, 1, False)
            scale = rounded_sum(m)
            high, low = split(by_lanes(by_rows(m)))
            back_y[plane, v] = jnp.concatenate([high, low[TILE:], low[:TILE]], axis=0)
            m = bands(v, plane, 0, False)
            scales.append(1.0 / (scale * rounded_sum(m)))
            m = by_lanes(reordered(m))
            fwd_x[plane, v] = m[:, :WIDE].astype(BF16)
            square = jnp.concatenate([m, jnp.zeros((LANES - WIDE, LANES), F32)], axis=0)
            high, low = split(square.T[:WIDE])
            side = high[:, TILE:].astype(F32)
            side = (side + turn(side, 64)).astype(BF16)
            for at, piece in (
                (0, high[:, :TILE]),
                (TILE, high[:, :TILE]),
                (2 * TILE, low[:, :TILE]),
                (3 * TILE, side),
                (3 * TILE + 128, low[:, TILE:]),
            ):
                back_x[plane, v, :, pl.ds(at, piece.shape[1])] = piece

    def forward(field, plane):
        field = field.astype(BF16)[:, :WIDE]
        along_y = dot(field, fwd_y[plane]).astype(BF16)
        return [
            dot(fwd_x[plane, v], along_y[:, v * LANES : (v + 1) * LANES])
            * scales[2 * plane + v]
            + background[v, plane]
            for v in range(2)
        ]

    def correction(ratios, plane, rows, lanes):
        total = jnp.zeros((rows, lanes), F32)
        for v in range(2):
            ratio = ratios[v].astype(BF16)
            ratio = jnp.concatenate([ratio, ratio[:, :TILE]], axis=1)
            high, low = split(dot(ratio, back_y[plane, v][:, :lanes]))
            stack = [high[:TILE], low[:TILE], high[:TILE], high[TILE:], low[TILE:], high[TILE:]]
            total = total + dot(
                back_x[plane, v][:rows, : 3 * WIDE], jnp.concatenate(stack, axis=0)
            )
        return total

    for plane in range(2):
        widen_estimate(plane)
        for v, blurred in enumerate(forward(wide_estimate[plane], plane)):
            inverse[plane, v] = 1.0 / blurred

    for plane in range(2):
        for v in range(2):
            for tile in range(2):
                measured[plane, v, tile, pl.ds(TILE, 8), :] = jnp.zeros((8, 128), F32)
                measured[plane, v, tile, pl.ds(WIDE - 8, 8), :] = jnp.zeros((8, 128), F32)

    rest = ids_in.at[pl.ds(1, DEVICES - 1)]
    pltpu.make_async_copy(rest, rest, ids_here).wait()
    ids_in[pl.ds(0, 1)] = ids_out[pl.ds(0, 1)]
    spot = iota((512, 256), 0).astype(F32)
    picked = (iota((8, 128), 1) // 16) == iota((8, 128), 0)
    for group in range(GROUPS):
        halves = []
        for half in range(2):
            eight = ids_in[pl.ds(group * GROUP + half * 8, 8)].reshape(8, 128)
            halves.append(jnp.sum(jnp.where(picked, eight, 0.0), axis=0, keepdims=True))
        wanted = jnp.concatenate(halves, axis=1)
        landing[:, pl.ds(group * 256, 256)] = jnp.where(spot == wanted, 1.0, 0.0).astype(BF16)

    def land(plane):
        incoming[plane, pl.ds(0, 16)] = outgoing[plane, pl.ds(0, 16)]
        for group in range(GROUPS):
            first = group * 256
            came = (
                incoming.at[plane, pl.ds(16, 240)]
                if group == 0
                else incoming.at[plane, pl.ds(first, 256)]
            )
            pltpu.make_async_copy(came, came, data_here.at[plane, group]).wait()
            part = dot(
                landing[:, pl.ds(first, 256)], incoming[plane, pl.ds(first, 256), :]
            )
            summed[...] = part if group == 0 else summed[...] + part
        send_sides(plane)
        group_of = narrow // 32
        for v in range(2):
            for h in range(2):
                for wide in range(2):
                    source = [
                        summed[
                            pl.ds(v * 256 + (wide * 4 + by) * 32, 32), pl.ds(h * 128, 128)
                        ]
                        for by in range(4)
                    ]
                    for x4 in range(4):
                        tile = source[x4]
                        for by in range(4):
                            if by != x4:
                                moved = pltpu.roll(source[by], ((by - x4) % 4) * 32, 1)
                                tile = jnp.where(group_of == by, moved, tile)
                        measured[plane, v, wide, pl.ds((h * 4 + x4) * 32, 32), :] = tile

    def wide_measured(plane, v):
        return jnp.concatenate([measured[plane, v, tile] for tile in range(3)], axis=1)

    def store(plane):
        return pltpu.make_async_copy(final.at[plane], result.at[plane], stored.at[plane])

    for plane in range(2):
        land(plane)
        send_others(plane)

    for plane in range(2):
        widen_measured(plane)
        ratios = [wide_measured(plane, v) * inverse[plane, v] for v in range(2)]
        current = wide_estimate[plane] * (0.5 * correction(ratios, plane, WIDE, LANES))
        ratios = [
            wide_measured(plane, v) / blurred for v, blurred in enumerate(forward(current, plane))
        ]
        final[plane] = current[:TILE, :TILE] * (
            0.5 * correction(ratios, plane, TILE, TILE)
        )
        store(plane).start()

    rest = ids_out.at[pl.ds(1, DEVICES - 1)]
    pltpu.make_async_copy(rest, rest, ids_sent).wait()
    for plane in range(2):
        rest = outgoing.at[plane, pl.ds(16, (DEVICES - 1) * 16)]
        pltpu.make_async_copy(rest, rest, data_sent.at[plane]).wait()
        whole = estimate_out.at[plane]
        pltpu.make_async_copy(whole, whole, estimate_sent.at[plane]).wait()
        whole = measured_out.at[plane]
        pltpu.make_async_copy(whole, whole, measured_sent.at[plane]).wait()
        store(plane).wait()


def shards(blocks, owner_route, block_slot, estimate, background, psf_taps, psf_index):
    owners = owner_route.reshape(owner_route.shape[:2])
    far = pl.BlockSpec(memory_space=pltpu.HBM)
    dma = pltpu.SemaphoreType.DMA
    return pl.pallas_call(
        kernel,
        out_shape=jax.ShapeDtypeStruct(estimate.shape, F32),
        in_specs=[far] * 7,
        out_specs=far,
        scratch_shapes=[
            pltpu.VMEM(blocks.shape, BF16),
            pltpu.VMEM(owners.shape, jnp.int32),
            pltpu.VMEM(block_slot.shape, jnp.int32),
            pltpu.VMEM(estimate.shape, F32),
            pltpu.SMEM(background.shape, F32),
            pltpu.SMEM(psf_taps.shape, F32),
            pltpu.SMEM(psf_index.shape, jnp.int32),
            pltpu.VMEM((2, 1024, 256), BF16),
            pltpu.VMEM((2, DEVICES * 16, 256), BF16),
            pltpu.VMEM((2, DEVICES * 16, 256), BF16),
            pltpu.VMEM((DEVICES, 1, 128), F32),
            pltpu.VMEM((DEVICES, 1, 128), F32),
            pltpu.VMEM((512, DEVICES * 16), BF16),
            pltpu.VMEM((512, 256), F32),
            pltpu.VMEM((2, WIDE, LANES), F32),
            pltpu.VMEM((2, 2, 3, WIDE, 128), F32),
            pltpu.VMEM((2, 2, WIDE, LANES), F32),
            pltpu.VMEM((2, TILE, TILE), F32),
            pltpu.VMEM((4, WIDE, 128), F32),
            pltpu.VMEM((2, ESTIMATE_ROWS, 128), BF16),
            pltpu.VMEM((2, ESTIMATE_ROWS, 128), BF16),
            pltpu.VMEM((2, MEASURED_ROWS, 128), BF16),
            pltpu.VMEM((2, MEASURED_ROWS, 128), BF16),
            pltpu.VMEM((2, WIDE, 2 * LANES), BF16),
            pltpu.VMEM((2, 2, WIDE, WIDE), BF16),
            pltpu.VMEM((2, 2, 2 * WIDE, LANES), BF16),
            pltpu.VMEM((2, 2, WIDE, 1024), BF16),
            pltpu.SemaphoreType.REGULAR,
            dma((7,)),
            dma((2,)),
            dma((2,)),
            dma((2, GROUPS)),
            dma,
            dma,
            dma((2,)),
            dma((2,)),
            dma((2,)),
            dma((2,)),
        ],
        compiler_params=pltpu.CompilerParams(
            collective_id=0, has_side_effects=True, vmem_limit_bytes=62 << 20
        ),
        cost_estimate=pl.CostEstimate(
            flops=8_000_000_000, bytes_accessed=2 << 20, transcendentals=0
        ),
    )(blocks, owners, block_slot, estimate, background, psf_taps, psf_index)


def solution(mesh):
    return jax.shard_map(
        shards,
        mesh=mesh,
        in_specs=(
            P(None, ("gx", "gy"), None),
            P(None, ("gx", "gy"), None),
            P(None, ("gx", "gy")),
            P(None, "gx", "gy"),
            P(),
            P(),
            P(),
        ),
        out_specs=P(None, "gx", "gy"),
        check_vma=False,
    )
```
